128 devices in a mesh: grp: 4 (over z_hi, core), dev: 32 (over z_lo, y, x).
Axes of the slice: x: 4, y: 4, z: 4 (z_hi: 2, z_lo: 2; z = z_hi * 2 + z_lo), core: 2. Of those that a mesh axis runs over, the one named last changes fastest.
Arguments:
- records: bfloat16 [1024, 16384], P('grp', 'dev'), may hold values from -30 to 30
- channel_map: int32 [4, 256], P('grp'), may hold values from 0 to 255, each once within a row
- source_offset: int32 [2, 128], P(None, ('grp', 'dev')), may hold values from 0 to 6
Outputs:
- correlations: bfloat16 [1, 512, 1024, 1024], P(None, None, ('grp', 'dev'))
The draws below stay inside these ranges and needn't reach their ends.
All inputs are finite; a program needn't handle non-finite values.
Results may differ from the reference program's by a relative error of at most 0.0075.
Values may be sent and summed in bfloat16 or wider, within the bound.
No kernel may reach another device: no remote copies, remote signals or barrier semaphores. Data moves between devices by JAX's collectives and lax.ppermute only.
A program may use at most 192 MiB of HBM per device.

```python
import math
import jax
import jax.numpy as jnp
from jax import lax

W = 2048
NLAG = 1024
STACKS = 1
SEGS = 8
CH_DEV = 8
SRC_DEV = 2
STEPS = 2
SRC = 256
TIME = 16384
CHG = 256
CH = 1024
N_GRP = 4
DEVICES = 128


def draw_records(key, part):
    key = jax.random.fold_in(key, 11)
    first = jax.random.fold_in(key, 0)
    noise = jax.random.normal(first, (CH, TIME), jnp.float32)
    return jnp.clip(noise, -6.0, 6.0).astype(jnp.bfloat16)


def place_ends(array, stream_key, smallest, high):
    shape = array.shape
    spot = [jax.random.randint(jax.random.fold_in(stream_key, axis), (), 0, shape[axis]) for axis in range(len(shape))]
    array = array.at[tuple(spot)].set(smallest)
    longest = shape.index(max(shape))
    spot[longest] = (spot[longest] + 1) % shape[longest]
    return array.at[tuple(spot)].set(high)


def setup_inputs(seed: int = 0) -> dict:
    keys = jax.random.split(jax.random.key(seed), 4)
    records = draw_records(jax.random.fold_in(keys[3], 71), 0)
    channel_map = jax.vmap(lambda own: jax.random.permutation(own, CHG))(jax.random.split(keys[1], N_GRP)).reshape((N_GRP, CHG)).astype(jnp.int32)
    source_offset = place_ends(jax.random.randint(keys[2], (STEPS, DEVICES), 0, CH_DEV - SRC_DEV + 1), jax.random.fold_in(keys[2], 1), 0, CH_DEV - SRC_DEV).astype(jnp.int32)
    return dict(records=records, channel_map=channel_map, source_offset=source_offset)


def tables(width, bin_count, lag_count):
    sample_index = jnp.arange(width, dtype=jnp.int32)[:, None]
    bin_index = jnp.arange(bin_count, dtype=jnp.int32)[None, :]
    phase_turns = sample_index * bin_index % width
    angles = phase_turns.astype(jnp.float32) * (2.0 * math.pi / width)
    forward = jnp.concatenate([jnp.cos(angles), -jnp.sin(angles)], axis=1).astype(jnp.bfloat16)
    lag_turns = (jnp.arange(lag_count, dtype=jnp.int32) - lag_count // 2) % width
    inv_turns = jnp.arange(bin_count, dtype=jnp.int32)[:, None] * lag_turns[None, :] % width
    inv_angles = inv_turns.astype(jnp.float32) * (2.0 * math.pi / width)
    inverse = jnp.concatenate([jnp.cos(inv_angles), -jnp.sin(inv_angles)], axis=0).astype(jnp.bfloat16)
    return (forward, inverse)

def whiten(spectra, kept_bins):
    real_part = spectra[:, :kept_bins]
    imag_part = spectra[:, kept_bins:]
    powers = real_part * real_part + imag_part * imag_part
    padded = jnp.pad(powers, ((0, 0), (4, 4)))
    smooth = padded[:, 0:kept_bins]
    for offset_bin in range(1, 9):
        smooth = smooth + padded[:, offset_bin:offset_bin + kept_bins]
    smooth = smooth / 9.0
    water_level = lax.optimization_barrier(jnp.mean(powers, axis=1, keepdims=True))
    inv_norm = lax.rsqrt(smooth + water_level + 1e-05)
    return jnp.concatenate([real_part * inv_norm, imag_part * inv_norm], axis=1)

def correlate(sources, resident, inverse, kept_bins):
    source_count = sources.shape[0]
    channels = resident.shape[0]
    src_view = sources.reshape(source_count, STACKS, SEGS, 2 * kept_bins).astype(jnp.float32)
    res_view = resident.reshape(channels, STACKS, SEGS, 2 * kept_bins).astype(jnp.float32)
    src_re, src_im = (src_view[..., :kept_bins], src_view[..., kept_bins:])
    res_re, res_im = (res_view[..., :kept_bins], res_view[..., kept_bins:])
    form = 'sqgk,cqgk->qsck'
    real_part = jnp.einsum(form, src_re, res_re) + jnp.einsum(form, src_im, res_im)
    imag_part = jnp.einsum(form, src_im, res_re) - jnp.einsum(form, src_re, res_im)
    factor = 2.0 / math.sqrt(SEGS * kept_bins)
    cross_spec = (factor * jnp.concatenate([real_part, imag_part], axis=-1)).astype(jnp.bfloat16)
    lagged = jnp.dot(cross_spec.reshape(-1, 2 * kept_bins), inverse, preferred_element_type=jnp.float32)
    return lagged.astype(jnp.bfloat16).reshape(STACKS, source_count, channels, -1)

def reference(records, channel_map, source_offset):
    kept_bins = W // 2
    forward, inverse = tables(W, kept_bins, NLAG)
    row_index = (jnp.arange(N_GRP, dtype=jnp.int32)[:, None] * CHG + channel_map).reshape(-1).astype(jnp.int32)
    ordered = jnp.take(records, row_index, axis=0)
    shard_count = CH // CH_DEV
    shards = ordered.reshape(shard_count, CH_DEV, TIME)

    def spec_block(shard_rows):
        spectra = jnp.dot(shard_rows.reshape(-1, W), forward, preferred_element_type=jnp.float32)
        return whiten(spectra, kept_bins).astype(jnp.bfloat16).reshape(CH_DEV, STACKS * SEGS, W)
    whitened = lax.map(spec_block, shards)
    flat = whitened.reshape(CH, STACKS * SEGS, W)
    picked = []
    for step_index in range(STEPS):
        base = jnp.arange(shard_count, dtype=jnp.int32)[:, None] * CH_DEV
        rows = base + source_offset[step_index].astype(jnp.int32)[:, None] + jnp.arange(SRC_DEV, dtype=jnp.int32)[None, :]
        picked.append(jnp.take(flat, rows.reshape(-1).astype(jnp.int32), axis=0))
    all_sources = jnp.concatenate(picked, axis=0)

    def corr_block(shard_spec):
        return correlate(all_sources, shard_spec, inverse, kept_bins)
    blocks = lax.map(corr_block, whitened)
    return jnp.transpose(blocks, (1, 2, 0, 3, 4)).reshape(STACKS, STEPS * SRC, CH, NLAG)
```

```python
import math

import jax
import jax.numpy as jnp
import numpy as np
from jax import lax
from jax.experimental import pallas as pl
from jax.experimental.pallas import tpu as pltpu
from jax.sharding import PartitionSpec as P

W = 2048
BINS = 1024
NLAG = 1024
SEGS = 8
CH_DEV = 8
SRC_DEV = 2
STEPS = 2
KIN = 16
BLK = SEGS * 2 * KIN
NBLK = BINS // KIN
WIDE = NBLK * BLK
HALF = WIDE // 2
AXES = ("grp", "dev")
MIB = 1 << 20
FACTOR = 2.0 / math.sqrt(SEGS * BINS)
OFFSETS = (0, -1, 1, 2)


def tables():
    turns = (np.arange(W)[:, None] * np.arange(BINS)[None, :]) % W
    angles = turns.astype(np.float32) * np.float32(2.0 * math.pi / W)
    forward = np.concatenate([np.cos(angles), -np.sin(angles)], axis=1)
    lag_turns = (np.arange(NLAG) - NLAG // 2) % W
    inv_turns = (np.arange(BINS)[:, None] * lag_turns[None, :]) % W
    inv_angles = inv_turns.astype(np.float32) * np.float32(2.0 * math.pi / W)
    inverse = np.concatenate([np.cos(inv_angles), -np.sin(inv_angles)], axis=0)
    return forward.astype(jnp.bfloat16), inverse.astype(jnp.bfloat16)


def chunk_transpose(vs):
    vs = list(vs)
    axis = vs[0].ndim - 1
    chunk = lax.broadcasted_iota(jnp.int32, vs[0].shape, axis) // 16
    for bit in (1, 2, 4):
        low = (chunk & bit) == 0
        for i in range(8):
            if i & bit == 0:
                a, b = vs[i], vs[i | bit]
                vs[i] = jnp.where(low, a, pltpu.roll(b, 16 * bit, axis))
                vs[i | bit] = jnp.where(low, pltpu.roll(a, 128 - 16 * bit, axis), b)
    return vs


def front_kernel(meta, rec, table, white, keep, send, spec, scr):
    total = None
    for q in range(4):
        x = rec[:, q].astype(jnp.float32).reshape(SEGS * CH_DEV, 512).astype(jnp.bfloat16)
        part = jnp.dot(x, table[q * 512 : (q + 1) * 512, :], preferred_element_type=jnp.float32)
        total = part if total is None else total + part
    re, im = total[:, :BINS], total[:, BINS:]
    power = re * re + im * im
    water = jnp.sum(power, axis=1, keepdims=True) * (1.0 / BINS)
    wide = jnp.concatenate([power, jnp.zeros((SEGS * CH_DEV, 128), jnp.float32)], axis=1)
    run = wide
    for shift in (1, 2, 4):
        run = run + pltpu.roll(run, shift, 1)
    run = run + pltpu.roll(wide, 8, 1)
    smooth = pltpu.roll(run, BINS + 128 - 4, 1)[:, :BINS] * (1.0 / 9.0)
    scale = lax.rsqrt(smooth + water + 1e-5)
    spec[:, :BINS] = re * scale
    spec[:, BINS:] = im * scale
    for kv in range(8):
        for h in range(2):
            vs = [
                spec[g * 8 : g * 8 + 8, ri * BINS + kv * 128 : ri * BINS + kv * 128 + 128]
                for g in range(4 * h, 4 * h + 4)
                for ri in range(2)
            ]
            for j, w in enumerate(chunk_transpose(vs)):
                at = (kv * 8 + j) * BLK + h * 128
                scr[:, at : at + 128] = w
    white[...] = scr[...].astype(jnp.bfloat16)
    core = meta[0]
    pair = lax.broadcasted_iota(jnp.int32, (CH_DEV, HALF), 0) // 2
    for out, half in ((keep, core), (send, 1 - core)):
        x = scr[:, pl.ds(pl.multiple_of(half * HALF, HALF), HALF)]
        a = jnp.where(pair == 2 * core, pltpu.roll(x, meta[1], 0), 0.0)
        b = jnp.where(pair == 2 * core + 1, pltpu.roll(x, meta[2], 0), 0.0)
        out[...] = (a + b).astype(jnp.bfloat16)


def front(meta, rec, table):
    vmem = pl.BlockSpec(memory_space=pltpu.VMEM)
    return pl.pallas_call(
        front_kernel,
        out_shape=(
            jax.ShapeDtypeStruct((CH_DEV, WIDE), jnp.bfloat16),
            jax.ShapeDtypeStruct((CH_DEV, HALF), jnp.bfloat16),
            jax.ShapeDtypeStruct((CH_DEV, HALF), jnp.bfloat16),
        ),
        in_specs=[pl.BlockSpec(memory_space=pltpu.SMEM), vmem, vmem],
        out_specs=(vmem, vmem, vmem),
        scratch_shapes=[
            pltpu.VMEM((SEGS * CH_DEV, 2 * BINS), jnp.float32),
            pltpu.VMEM((CH_DEV, WIDE), jnp.float32),
        ],
        compiler_params=pltpu.CompilerParams(vmem_limit_bytes=32 * MIB),
        name="front",
    )(meta, rec, table)


def corr_kernel(
    first, meta, b_ref, m0, m1, m2, m3, sib, e_hbm, *rest
):
    out, rows_scr, x_scr, e_scr, ov, yf, yb, sems = rest if first else rest[1:]
    e_copy = pltpu.make_async_copy(e_hbm, e_scr, sems.at[0])
    e_copy.start()
    core = meta[0]
    own = b_ref[...].astype(jnp.float32)
    lane = lax.broadcasted_iota(jnp.int32, (CH_DEV, WIDE), 1)
    turned = jnp.where(
        (lane & 16) == 0, -pltpu.roll(own, WIDE - 16, 1), pltpu.roll(own, 16, 1)
    )
    rows_scr[0:8, :] = own
    rows_scr[8:16, :] = turned
    diag = lax.broadcasted_iota(jnp.int32, (KIN, BLK), 0) == (
        lax.broadcasted_iota(jnp.int32, (KIN, BLK), 1) & 15
    )

    def group(j, mine):
        half = core if mine else 1 - core
        g = half * 4 + j
        for i in range(8):
            lanes = pl.ds(pl.multiple_of((j * 8 + i) * BLK, BLK), BLK)
            if mine:
                a = jnp.concatenate([m[:, lanes] for m in (m0, m1, m2, m3)], axis=0)
            else:
                a = sib[:, lanes]
            r = rows_scr[:, pl.ds(pl.multiple_of((g * 8 + i) * BLK, BLK), BLK)]
            block = jnp.where(diag[None], r[:, None, :], 0.0).astype(jnp.bfloat16)
            block = block.reshape(2 * CH_DEV * KIN, BLK)
            prod = lax.dot_general(
                a, block, (((1,), (1,)), ((), ())), preferred_element_type=jnp.float32
            )
            ov[i] = prod * FACTOR
        for ri in range(2):
            at = pl.ds(pl.multiple_of(ri * BINS + g * 128, 128), 128)
            for rb in range(8):
                if mine:
                    vs = [ov[i, rb * 16 : rb * 16 + 16, ri * 128 : ri * 128 + 128] for i in range(8)]
                else:
                    n0, n1 = 2 * rb, 2 * rb + 1
                    s0 = ((n0 % 4) * 4 + n0 // 4) * 8
                    s1 = ((n1 % 4) * 4 + n1 // 4) * 8
                    vs = [
                        jnp.concatenate(
                            [
                                ov[i, s0 : s0 + 8, ri * 128 : ri * 128 + 128],
                                ov[i, s1 : s1 + 8, ri * 128 : ri * 128 + 128],
                            ],
                            axis=0,
                        )
                        for i in range(8)
                    ]
                for c, w in enumerate(chunk_transpose(vs)):
                    x_scr[c * 128 + rb * 16 : c * 128 + rb * 16 + 16, at] = w.astype(jnp.bfloat16)

    @pl.loop(0, 4)
    def _(j):
        group(j, True)

    @pl.loop(0, 4)
    def _(j):
        group(j, False)

    e_copy.wait()

    @pl.loop(0, 4)
    def _(n):
        lanes = pl.ds(pl.multiple_of(n * 256, 256), 256)
        y = jnp.dot(x_scr[...], e_scr[:, lanes], preferred_element_type=jnp.float32)
        for c in range(CH_DEV):
            for h in range(2):
                yf[h, pl.ds(c, 128, stride=8), :] = y[c * 128 : c * 128 + 128, h * 128 : h * 128 + 128]
        for h in range(2):
            lanes = pl.ds(pl.multiple_of(n * 256 + h * 128, 128), 128)
            yb[:, lanes] = yf[h].astype(jnp.bfloat16)

    def copy(n):
        return pltpu.make_async_copy(
            yb.at[pl.ds(pl.multiple_of(n * 16, 16), 16)],
            out.at[pl.ds(pl.multiple_of(meta[1 + n] * 16, 16), 16)],
            sems.at[1],
        )

    @pl.loop(0, 64)
    def _(n):
        copy(n).start()

    @pl.loop(0, 64)
    def _(n):
        copy(n).wait()


def corr(meta, white, mine, sib, inverse, out):
    first = out is None
    vmem = pl.BlockSpec(memory_space=pltpu.VMEM)
    anym = pl.BlockSpec(memory_space=pl.ANY)
    args = [meta, white, *mine, sib, inverse] + ([] if first else [out])
    return pl.pallas_call(
        lambda *refs: corr_kernel(first, *refs),
        out_shape=jax.ShapeDtypeStruct((STEPS * 256 * CH_DEV, NLAG), jnp.bfloat16),
        in_specs=[pl.BlockSpec(memory_space=pltpu.SMEM)] + [vmem] * 6 + [anym] * (len(args) - 7),
        out_specs=anym,
        scratch_shapes=[
            pltpu.VMEM((16, WIDE), jnp.float32),
            pltpu.VMEM((1024, 2 * BINS), jnp.bfloat16),
            pltpu.VMEM((2 * BINS, NLAG), jnp.bfloat16),
            pltpu.VMEM((8, 128, 256), jnp.float32),
            pltpu.VMEM((2, 1024, 128), jnp.float32),
            pltpu.VMEM((1024, NLAG), jnp.bfloat16),
            pltpu.SemaphoreType.DMA((2,)),
        ],
        input_output_aliases={} if first else {8: 0},
        compiler_params=pltpu.CompilerParams(vmem_limit_bytes=40 * MIB),
        cost_estimate=pl.CostEstimate(
            flops=7 * 1024 * 2048 * 1024, bytes_accessed=12 * MIB, transcendentals=0
        ),
        name="corr",
    )(*args)


def device(x, y, z, core):
    return ((z // 2) * 2 + core) * 32 + (z % 2) * 16 + y * 4 + x


def line_pairs(axes, step):
    pairs = []
    for core in range(2):
        for n in range(64):
            at = {"x": n % 4, "y": n // 4 % 4, "z": n // 16}
            to = dict(at)
            to[axes[core]] = (at[axes[core]] + step) % 4
            pairs.append((device(**at, core=core), device(**to, core=core)))
    return pairs


CORE_PAIRS = [
    (device(n % 4, n // 4 % 4, n // 16, core), device(n % 4, n // 4 % 4, n // 16, 1 - core))
    for core in range(2)
    for n in range(64)
]


def line(block, axes):
    return [block] + [lax.ppermute(block, AXES, line_pairs(axes, s)) for s in (1, -1, 2)]


def local(records, channel_map, source_offset):
    forward, inverse = tables()
    forward, inverse = jnp.asarray(forward), jnp.asarray(inverse)
    grp, dev = lax.axis_index("grp"), lax.axis_index("dev")
    core = grp % 2
    x0, y0, z0 = dev % 4, dev // 4 % 4, (grp // 2) * 2 + dev // 16

    pick = (channel_map[0][:, None] == jnp.arange(256, dtype=jnp.int32)[None, :]).astype(jnp.bfloat16)
    ordered = jnp.dot(pick, records, preferred_element_type=jnp.float32).astype(jnp.bfloat16)
    regrouped = lax.all_to_all(ordered.reshape(32, 8, 512), "dev", split_axis=0, concat_axis=0, tiled=True)

    turns = (4 * core + 2 * jnp.arange(2, dtype=jnp.int32) - source_offset[:, 0]) % 8
    front_meta = jnp.stack([core, turns[0], turns[1]])
    white, keep, send = front(front_meta, regrouped.reshape(8, 4, 8, 512), forward)
    block = keep + lax.ppermute(send, AXES, CORE_PAIRS)

    near = jnp.concatenate(line(block[None], "xz"), axis=0)
    lines = line(near, "yy")
    off = jnp.array(OFFSETS, jnp.int32)
    outer, inner = jnp.meshgrid(off, off, indexing="ij")
    xs = (x0 + jnp.where(core == 0, inner, outer)) % 4
    zs = (z0 + jnp.where(core == 0, outer, inner)) % 4
    out = None
    for k in range(4):
        ys = (y0 + OFFSETS[k]) % 4
        chip = (zs // 2) * 64 + (zs % 2) * 16 + ys * 4 + xs
        place = chip.reshape(16, 1, 1) + jnp.arange(2)[None, :, None] * 32 + jnp.arange(2)[None, None, :] * 128
        meta = jnp.concatenate([core[None], place.reshape(64)]).astype(jnp.int32)
        mine = line(lines[k], "zx")
        sib = lax.ppermute(jnp.concatenate(mine, axis=0), AXES, CORE_PAIRS)
        out = corr(meta, white, [m.reshape(32, HALF) for m in mine], sib.reshape(128, HALF), inverse, out)
    return out.reshape(1, STEPS * 256, CH_DEV, NLAG)


def solution(mesh):
    return jax.shard_map(
        local,
        mesh=mesh,
        in_specs=(P("grp", "dev"), P("grp", None), P(None, ("grp", "dev"))),
        out_specs=P(None, None, ("grp", "dev"), None),
        check_vma=False,
    )
```

```python
import math

import jax
import jax.numpy as jnp
import numpy as np
from jax import lax
from jax.experimental import pallas as pl
from jax.experimental.pallas import tpu as pltpu
from jax.sharding import PartitionSpec as P

W = 2048
BINS = 1024
NLAG = 1024
SEGS = 8
CH_DEV = 8
SRC_DEV = 2
STEPS = 2
KIN = 16
BLK = SEGS * 2 * KIN
NBLK = BINS // KIN
WIDE = NBLK * BLK
HALF = WIDE // 2
GROUP = 8 * BLK
NB = 1
CB = 8 // NB
AXES = ("grp", "dev")
MIB = 1 << 20
FACTOR = 2.0 / math.sqrt(SEGS * BINS)
OFFSETS = (0, -1, 1, 2)


def tables():
    turns = (np.arange(W)[:, None] * np.arange(BINS)[None, :]) % W
    angles = turns.astype(np.float32) * np.float32(2.0 * math.pi / W)
    forward = np.concatenate([np.cos(angles), -np.sin(angles)], axis=1)
    lag_turns = (np.arange(NLAG) - NLAG // 2) % W
    inv_turns = (np.arange(BINS)[:, None] * lag_turns[None, :]) % W
    inv_angles = inv_turns.astype(np.float32) * np.float32(2.0 * math.pi / W)
    inverse = np.concatenate([np.cos(inv_angles), -np.sin(inv_angles)], axis=0)
    return forward.astype(jnp.bfloat16), inverse.astype(jnp.bfloat16)


def chunk_transpose(vs):
    vs = list(vs)
    axis = vs[0].ndim - 1
    chunk = lax.broadcasted_iota(jnp.int32, vs[0].shape, axis) // 16
    for bit in (1, 2, 4):
        low = (chunk & bit) == 0
        for i in range(8):
            if i & bit == 0:
                a, b = vs[i], vs[i | bit]
                vs[i] = jnp.where(low, a, pltpu.roll(b, 16 * bit, axis))
                vs[i | bit] = jnp.where(low, pltpu.roll(a, 128 - 16 * bit, axis), b)
    return vs


def front_kernel(meta, rec, table_hbm, white, keep, send, spec, scr, table, sems):
    def load(q):
        rows = pl.ds(q * 512, 512)
        return pltpu.make_async_copy(table_hbm.at[rows], table.at[rows], sems.at[q])

    for q in range(4):
        load(q).start()
    total = None
    for q in range(4):
        load(q).wait()
        x = rec[:, q].astype(jnp.float32).reshape(SEGS * CH_DEV, 512).astype(jnp.bfloat16)
        part = jnp.dot(x, table[q * 512 : (q + 1) * 512, :], preferred_element_type=jnp.float32)
        total = part if total is None else total + part
    re, im = total[:, :BINS], total[:, BINS:]
    power = re * re + im * im
    water = jnp.sum(power, axis=1, keepdims=True) * (1.0 / BINS)
    wide = jnp.concatenate([power, jnp.zeros((SEGS * CH_DEV, 128), jnp.float32)], axis=1)
    run = wide
    for shift in (1, 2, 4):
        run = run + pltpu.roll(run, shift, 1)
    run = run + pltpu.roll(wide, 8, 1)
    smooth = pltpu.roll(run, BINS + 128 - 4, 1)[:, :BINS] * (1.0 / 9.0)
    scale = lax.rsqrt(smooth + water + 1e-5)
    spec[:, :BINS] = re * scale
    spec[:, BINS:] = im * scale
    for kv in range(8):
        for h in range(2):
            vs = [
                spec[g * 8 : g * 8 + 8, ri * BINS + kv * 128 : ri * BINS + kv * 128 + 128]
                for g in range(4 * h, 4 * h + 4)
                for ri in range(2)
            ]
            for j, w in enumerate(chunk_transpose(vs)):
                at = (kv * 8 + j) * BLK + h * 128
                scr[:, at : at + 128] = w
    white[...] = scr[...].astype(jnp.bfloat16)
    core = meta[0]
    pair = lax.broadcasted_iota(jnp.int32, (CH_DEV, HALF), 0) // 2
    for out, half in ((keep, core), (send, 1 - core)):
        x = scr[:, pl.ds(pl.multiple_of(half * HALF, HALF), HALF)]
        a = jnp.where(pair == 2 * core, pltpu.roll(x, meta[1], 0), 0.0)
        b = jnp.where(pair == 2 * core + 1, pltpu.roll(x, meta[2], 0), 0.0)
        out[...] = (a + b).astype(jnp.bfloat16)


def front(meta, rec, table):
    vmem = pl.BlockSpec(memory_space=pltpu.VMEM)
    return pl.pallas_call(
        front_kernel,
        out_shape=(
            jax.ShapeDtypeStruct((CH_DEV, WIDE), jnp.bfloat16),
            jax.ShapeDtypeStruct((CH_DEV, HALF), jnp.bfloat16),
            jax.ShapeDtypeStruct((CH_DEV, HALF), jnp.bfloat16),
        ),
        in_specs=[pl.BlockSpec(memory_space=pltpu.SMEM), vmem, pl.BlockSpec(memory_space=pltpu.MemorySpace.HBM)],
        out_specs=(vmem, vmem, vmem),
        scratch_shapes=[
            pltpu.VMEM((SEGS * CH_DEV, 2 * BINS), jnp.float32),
            pltpu.VMEM((CH_DEV, WIDE), jnp.float32),
            pltpu.VMEM((W, 2 * BINS), jnp.bfloat16),
            pltpu.SemaphoreType.DMA((4,)),
        ],
        compiler_params=pltpu.CompilerParams(vmem_limit_bytes=60 * MIB),
        name="front",
    )(meta, rec, table)


def corr_kernel(first, meta, b_ref, *refs):
    mine, sib, e_hbm = refs[:4], refs[4:8], refs[8]
    out, rows_scr, a_scr, x_scr, e_scr, ov, yf, yb, a_sems, sems = refs[9 if first else 10 :]

    def load(j, half, n):
        return pltpu.make_async_copy(
            (mine, sib)[half][n].at[:, pl.ds(pl.multiple_of(j * GROUP, GROUP), GROUP)],
            a_scr.at[half, j, pl.ds(n * 32, 32)],
            a_sems.at[half, j],
        )

    for j in range(4):
        for half in range(2):
            for n in range(4):
                load(j, half, n).start()
    e_copy = pltpu.make_async_copy(e_hbm, e_scr, sems.at[0])
    e_copy.start()
    core = meta[0]
    own = b_ref[...].astype(jnp.float32)
    lane = lax.broadcasted_iota(jnp.int32, (CH_DEV, WIDE), 1)
    turned = jnp.where(
        (lane & 16) == 0, -pltpu.roll(own, WIDE - 16, 1), pltpu.roll(own, 16, 1)
    )
    for p in range(NB):
        rows_scr[p, 0:CB, :] = own[CB * p : CB * p + CB]
        rows_scr[p, CB : 2 * CB, :] = turned[CB * p : CB * p + CB]
    diag = lax.broadcasted_iota(jnp.int32, (KIN, BLK), 0) == (
        lax.broadcasted_iota(jnp.int32, (KIN, BLK), 1) & 15
    )

    def group(p, j, half):
        g = (core if half == 0 else 1 - core) * 4 + j
        for i in range(8):
            a = a_scr[half, j, :, i * BLK : i * BLK + BLK]
            if half == 1:
                a = jnp.concatenate(
                    [a[32 * n + 8 * o : 32 * n + 8 * o + 8] for o in range(4) for n in range(4)], axis=0
                )
            r = rows_scr[p, :, pl.ds(pl.multiple_of((g * 8 + i) * BLK, BLK), BLK)]
            block = jnp.where(diag[None], r[:, None, :], 0.0).astype(jnp.bfloat16)
            prod = lax.dot_general(
                block.reshape(2 * CB * KIN, BLK), a, (((1,), (1,)), ((), ())), preferred_element_type=jnp.float32
            )
            prod = (prod * FACTOR).astype(jnp.bfloat16)
            ov[half, :, i * KIN : (i + 1) * KIN, :] = prod.reshape(2 * CB, KIN, 128)
        for ri in range(2):
            at = pl.ds(pl.multiple_of(ri * BINS + g * 128, 128), 128)
            for c in range(CB):
                x_scr[p % 2, c * 128 : c * 128 + 128, at] = ov[half, ri * CB + c].T

    def lags(p, n):
        y = jnp.dot(
            x_scr[p % 2],
            e_scr[:, pl.ds(pl.multiple_of(n * 256, 256), 256)],
            preferred_element_type=jnp.float32,
        )
        for c in range(CB):
            for h in range(2):
                yf[2 * n + h, pl.ds(CB * p + c, 128, stride=8), :] = y[c * 128 : c * 128 + 128, h * 128 : h * 128 + 128]

    for p in range(NB + 1):

        @pl.loop(0, 4)
        def _(j):
            if p == 0:
                for half in range(2):
                    for n in range(4):
                        load(j, half, n).wait()
            if p > 0:
                lags(p - 1, j)
            if p < NB:
                group(p, j, 0)
                group(p, j, 1)
            if p == NB:
                for h in range(2):
                    lanes = pl.ds(pl.multiple_of(j * 256 + h * 128, 128), 128)
                    yb[:, lanes] = yf[2 * j + h].astype(jnp.bfloat16)

        if p == 0:
            e_copy.wait()

    def copy(n):
        return pltpu.make_async_copy(
            yb.at[pl.ds(pl.multiple_of(n * 16, 16), 16)],
            out.at[pl.ds(pl.multiple_of(meta[1 + n] * 16, 16), 16)],
            sems.at[1],
        )

    @pl.loop(0, 64)
    def _(n):
        copy(n).start()

    @pl.loop(0, 64)
    def _(n):
        copy(n).wait()


def corr(meta, white, mine, sib, inverse, out):
    first = out is None
    vmem = pl.BlockSpec(memory_space=pltpu.VMEM)
    hbm = pl.BlockSpec(memory_space=pltpu.MemorySpace.HBM)
    args = [meta, white, *mine, *sib, inverse] + ([] if first else [out])
    return pl.pallas_call(
        lambda *refs: corr_kernel(first, *refs),
        out_shape=jax.ShapeDtypeStruct((STEPS * 256 * CH_DEV, NLAG), jnp.bfloat16),
        in_specs=[pl.BlockSpec(memory_space=pltpu.SMEM), vmem] + [hbm] * (len(args) - 2),
        out_specs=hbm,
        scratch_shapes=[
            pltpu.VMEM((NB, 2 * CB, WIDE), jnp.float32),
            pltpu.VMEM((2, 4, 128, GROUP), jnp.bfloat16),
            pltpu.VMEM((min(NB, 2), CB * 128, 2 * BINS), jnp.bfloat16),
            pltpu.VMEM((2 * BINS, NLAG), jnp.bfloat16),
            pltpu.VMEM((2, 2 * CB, 128, 128), jnp.bfloat16),
            pltpu.VMEM((8, 1024, 128), jnp.float32),
            pltpu.VMEM((1024, NLAG), jnp.bfloat16),
            pltpu.SemaphoreType.DMA((2, 4)),
            pltpu.SemaphoreType.DMA((2,)),
        ],
        input_output_aliases={} if first else {11: 0},
        compiler_params=pltpu.CompilerParams(vmem_limit_bytes=60 * MIB),
        cost_estimate=pl.CostEstimate(
            flops=7 * 1024 * 2048 * 1024, bytes_accessed=12 * MIB, transcendentals=0
        ),
        name="corr",
    )(*args)


def device(x, y, z, core):
    return ((z // 2) * 2 + core) * 32 + (z % 2) * 16 + y * 4 + x


def line_pairs(axes, step):
    pairs = []
    for core in range(2):
        for n in range(64):
            at = {"x": n % 4, "y": n // 4 % 4, "z": n // 16}
            to = dict(at)
            to[axes[core]] = (at[axes[core]] + step) % 4
            pairs.append((device(**at, core=core), device(**to, core=core)))
    return pairs


CORE_PAIRS = [
    (device(n % 4, n // 4 % 4, n // 16, core), device(n % 4, n // 4 % 4, n // 16, 1 - core))
    for core in range(2)
    for n in range(64)
]


def line(block, axes):
    return [block] + [lax.ppermute(block, AXES, line_pairs(axes, s)) for s in (1, -1, 2)]


def local(records, channel_map, source_offset):
    forward, inverse = tables()
    forward, inverse = jnp.asarray(forward), jnp.asarray(inverse)
    grp, dev = lax.axis_index("grp"), lax.axis_index("dev")
    core = grp % 2
    x0, y0, z0 = dev % 4, dev // 4 % 4, (grp // 2) * 2 + dev // 16

    pick = (channel_map[0][:, None] == jnp.arange(256, dtype=jnp.int32)[None, :]).astype(jnp.bfloat16)
    ordered = jnp.dot(pick, records, preferred_element_type=jnp.float32).astype(jnp.bfloat16)
    regrouped = lax.all_to_all(ordered.reshape(32, 8, 512), "dev", split_axis=0, concat_axis=0, tiled=True)

    turns = (4 * core + 2 * jnp.arange(2, dtype=jnp.int32) - source_offset[:, 0]) % 8
    front_meta = jnp.stack([core, turns[0], turns[1]])
    white, keep, send = front(front_meta, regrouped.reshape(8, 4, 8, 512), forward)
    block = keep + lax.ppermute(send, AXES, CORE_PAIRS)

    near = jnp.concatenate(line(block[None], "xz"), axis=0)
    mine = line(near, "zx")
    ahead, behind = (lax.ppermute(near, AXES, line_pairs("yy", s)) for s in (1, -1))
    off = jnp.array(OFFSETS, jnp.int32)
    outer, inner = jnp.meshgrid(off, off, indexing="ij")
    xs = (x0 + jnp.where(core == 0, inner, outer)) % 4
    zs = (z0 + jnp.where(core == 0, outer, inner)) % 4
    out = None
    after = lax.optimization_barrier
    for k in range(4):
        ys = (y0 + OFFSETS[k]) % 4
        chip = (zs // 2) * 64 + (zs % 2) * 16 + ys * 4 + xs
        place = chip.reshape(16, 1, 1) + jnp.arange(2)[None, :, None] * 32 + jnp.arange(2)[None, None, :] * 128
        meta = jnp.concatenate([core[None], place.reshape(64)]).astype(jnp.int32)
        now = mine
        if k > 0:
            out, *now = after((out, *now))
        sib = [lax.ppermute(m, AXES, CORE_PAIRS) for m in now]
        if k == 0:
            near, ahead, *now = after((near, ahead, *now))
            mine = line(ahead, "zx")
            across = lax.ppermute(near, AXES, line_pairs("yy", 2))
        elif k == 1:
            behind, *now = after((behind, *now))
            mine = line(behind, "zx")
        elif k == 2:
            across, *now = after((across, *now))
            mine = line(across, "zx")
        flat = lambda ms: [m.reshape(32, HALF) for m in ms]
        out = corr(meta, white, flat(now), flat(sib), inverse, out)
    return out.reshape(1, STEPS * 256, CH_DEV, NLAG)


def solution(mesh):
    return jax.shard_map(
        local,
        mesh=mesh,
        in_specs=(P("grp", "dev"), P("grp", None), P(None, ("grp", "dev"))),
        out_specs=P(None, None, ("grp", "dev"), None),
        check_vma=False,
    )
```

```python
import math

import jax
import jax.numpy as jnp
import numpy as np
from jax import lax
from jax.experimental import pallas as pl
from jax.experimental.pallas import tpu as pltpu
from jax.sharding import PartitionSpec as P

W = 2048
BINS = 1024
NLAG = 1024
SEGS = 8
CH_DEV = 8
SRC_DEV = 2
STEPS = 2
KIN = 16
BLK = SEGS * 2 * KIN
NBLK = BINS // KIN
WIDE = NBLK * BLK
HALF = WIDE // 2
GROUP = 8 * BLK
AXES = ("grp", "dev")
MIB = 1 << 20
FACTOR = 2.0 / math.sqrt(SEGS * BINS)
OFFSETS = (0, -1, 1, 2)


def tables():
    turns = (np.arange(W)[:, None] * np.arange(BINS)[None, :]) % W
    angles = turns.astype(np.float32) * np.float32(2.0 * math.pi / W)
    forward = np.concatenate([np.cos(angles), -np.sin(angles)], axis=1)
    inv_turns = (np.arange(BINS)[:, None] * np.arange(NLAG // 2)[None, :]) % W
    inv_angles = inv_turns.astype(np.float32) * np.float32(2.0 * math.pi / W)
    inverse = np.concatenate([np.cos(inv_angles), -np.sin(inv_angles)], axis=0)
    return forward.astype(jnp.bfloat16), inverse.astype(jnp.bfloat16)


def chunk_transpose(vs):
    vs = list(vs)
    axis = vs[0].ndim - 1
    chunk = lax.broadcasted_iota(jnp.int32, vs[0].shape, axis) // 16
    for bit in (1, 2, 4):
        low = (chunk & bit) == 0
        for i in range(8):
            if i & bit == 0:
                a, b = vs[i], vs[i | bit]
                vs[i] = jnp.where(low, a, pltpu.roll(b, 16 * bit, axis))
                vs[i | bit] = jnp.where(low, pltpu.roll(a, 128 - 16 * bit, axis), b)
    return vs


def front_kernel(meta, rec, table_hbm, white, keep, send, spec, scr, table, sems):
    def load(n):
        rows = pl.ds(n * 256, 256)
        return pltpu.make_async_copy(table_hbm.at[rows], table.at[rows], sems.at[n])

    for n in range(8):
        load(n).start()
    total = None
    for q in range(4):
        x = rec[:, q].astype(jnp.float32).reshape(SEGS * CH_DEV, 512).astype(jnp.bfloat16)
        for h in range(2):
            n = 2 * q + h
            load(n).wait()
            part = jnp.dot(
                x[:, h * 256 : h * 256 + 256], table[n * 256 : n * 256 + 256, :], preferred_element_type=jnp.float32
            )
            total = part if total is None else total + part
    re, im = total[:, :BINS], total[:, BINS:]
    power = re * re + im * im
    water = jnp.sum(power, axis=1, keepdims=True) * (1.0 / BINS)
    wide = jnp.concatenate([power, jnp.zeros((SEGS * CH_DEV, 128), jnp.float32)], axis=1)
    run = wide
    for shift in (1, 2, 4):
        run = run + pltpu.roll(run, shift, 1)
    run = run + pltpu.roll(wide, 8, 1)
    smooth = pltpu.roll(run, BINS + 128 - 4, 1)[:, :BINS] * (1.0 / 9.0)
    scale = lax.rsqrt(smooth + water + 1e-5)
    spec[:, :BINS] = re * scale
    spec[:, BINS:] = im * scale
    for kv in range(8):
        for h in range(2):
            vs = [
                spec[g * 8 : g * 8 + 8, ri * BINS + kv * 128 : ri * BINS + kv * 128 + 128]
                for g in range(4 * h, 4 * h + 4)
                for ri in range(2)
            ]
            for j, w in enumerate(chunk_transpose(vs)):
                at = (kv * 8 + j) * BLK + h * 128
                scr[:, at : at + 128] = w
    white[...] = scr[...].astype(jnp.bfloat16)
    core = meta[0]
    pair = lax.broadcasted_iota(jnp.int32, (CH_DEV, HALF), 0) // 2
    for out, half in ((keep, core), (send, 1 - core)):
        x = scr[:, pl.ds(pl.multiple_of(half * HALF, HALF), HALF)]
        a = jnp.where(pair == 2 * core, pltpu.roll(x, meta[1], 0), 0.0)
        b = jnp.where(pair == 2 * core + 1, pltpu.roll(x, meta[2], 0), 0.0)
        out[...] = (a + b).astype(jnp.bfloat16)


def front(meta, rec, table):
    vmem = pl.BlockSpec(memory_space=pltpu.VMEM)
    return pl.pallas_call(
        front_kernel,
        out_shape=(
            jax.ShapeDtypeStruct((CH_DEV, WIDE), jnp.bfloat16),
            jax.ShapeDtypeStruct((CH_DEV, HALF), jnp.bfloat16),
            jax.ShapeDtypeStruct((CH_DEV, HALF), jnp.bfloat16),
        ),
        in_specs=[pl.BlockSpec(memory_space=pltpu.SMEM), vmem, pl.BlockSpec(memory_space=pltpu.MemorySpace.HBM)],
        out_specs=(vmem, vmem, vmem),
        scratch_shapes=[
            pltpu.VMEM((SEGS * CH_DEV, 2 * BINS), jnp.float32),
            pltpu.VMEM((CH_DEV, WIDE), jnp.float32),
            pltpu.VMEM((W, 2 * BINS), jnp.bfloat16),
            pltpu.SemaphoreType.DMA((8,)),
        ],
        compiler_params=pltpu.CompilerParams(vmem_limit_bytes=60 * MIB),
        name="front",
    )(meta, rec, table)


def rows_kernel(white, rows):
    own = white[...].astype(jnp.float32)
    lane = lax.broadcasted_iota(jnp.int32, (CH_DEV, WIDE), 1)
    turned = jnp.where(
        (lane & 16) == 0, -pltpu.roll(own, WIDE - 16, 1), pltpu.roll(own, 16, 1)
    )
    last = jnp.where((lane & 1) == 0, own, turned)
    last = jnp.where((lane & 2) == 0, last, -last)
    parts = [own, turned, last, jnp.zeros_like(own)]
    rows[...] = jnp.concatenate(parts, axis=0).astype(jnp.bfloat16)


def channel_rows(white):
    vmem = pl.BlockSpec(memory_space=pltpu.VMEM)
    return pl.pallas_call(
        rows_kernel,
        out_shape=jax.ShapeDtypeStruct((4 * CH_DEV, WIDE), jnp.bfloat16),
        in_specs=[vmem],
        out_specs=vmem,
        compiler_params=pltpu.CompilerParams(vmem_limit_bytes=16 * MIB),
        name="rows",
    )(white)


def corr_kernel(first, planes, arrays, meta, rows_hbm, *refs):
    pieces, sources = 4 * planes, 128 * planes
    mine, sib, e_hbm = refs[:arrays], refs[arrays : 2 * arrays], refs[2 * arrays]
    out, rows_scr, a_scr, x_scr, e_scr, flip, ov, edge, edge_t, d_scr, yf, yb, a_sems, sems = refs[2 * arrays + (1 if first else 2) :]

    def load(j, half, n):
        lines = (mine, sib)[half]
        if len(lines) == pieces:
            ref, row = lines[n], 0
        elif n % 4 < 3:
            ref, row = lines[n % 4], n // 4 * 32
        else:
            ref, row = lines[3 + n // 4], 0
        return pltpu.make_async_copy(
            ref.at[pl.ds(row, 32), pl.ds(pl.multiple_of(j * GROUP, GROUP), GROUP)],
            a_scr.at[half, j, pl.ds(n * 32, 32)],
            a_sems.at[half, j],
        )

    def load_rows(j, half):
        g = (core if half == 0 else 1 - core) * 4 + j
        return pltpu.make_async_copy(
            rows_hbm.at[:, pl.ds(pl.multiple_of(g * GROUP, GROUP), GROUP)],
            rows_scr.at[half, j],
            a_sems.at[half, j],
        )

    core = meta[0]
    for j in range(4):
        for half in range(2):
            load_rows(j, half).start()
            for n in range(pieces):
                load(j, half, n).start()
    e_copy = pltpu.make_async_copy(e_hbm, e_scr, sems.at[0])
    e_copy.start()
    diag = lax.broadcasted_iota(jnp.int32, (KIN, BLK), 0) == (
        lax.broadcasted_iota(jnp.int32, (KIN, BLK), 1) & 15
    )
    back = lax.broadcasted_iota(jnp.int32, (512, 512), 0) + lax.broadcasted_iota(jnp.int32, (512, 512), 1)
    flip[...] = jnp.where(back == 512, 1.0, 0.0).astype(jnp.bfloat16)
    edge[...] = jnp.zeros((128, sources), jnp.float32)

    def group(j, half):
        g = (core if half == 0 else 1 - core) * 4 + j
        for i in range(8):
            a = a_scr[half, j, :, i * BLK : i * BLK + BLK]
            if half == 1:
                a = jnp.concatenate(
                    [
                        a[128 * k + 32 * n + 8 * o : 128 * k + 32 * n + 8 * o + 8]
                        for k in range(planes)
                        for o in range(4)
                        for n in range(4)
                    ],
                    axis=0,
                )
            r = rows_scr[half, j, :, i * BLK : i * BLK + BLK].astype(jnp.float32)
            block = jnp.where(diag[None], r[:16, None, :], 0.0).astype(jnp.bfloat16)
            block = jnp.concatenate([block.reshape(256, BLK), r[16:].astype(jnp.bfloat16)], axis=0)
            prod = lax.dot_general(
                block, a, (((1,), (1,)), ((), ())), preferred_element_type=jnp.float32
            )
            prod = prod * FACTOR
            edge[0:8, :] += prod[256:264]
            ov[half, :, i * KIN : (i + 1) * KIN, :] = prod[:256].astype(jnp.bfloat16).reshape(16, KIN, sources)
        for ri in range(2):
            at = pl.ds(pl.multiple_of(ri * BINS + g * 128, 128), 128)
            for c in range(CH_DEV):
                x_scr[:, c, :, at] = ov[half, ri * 8 + c].T.reshape(2 * planes, 64, 128)

    @pl.loop(0, 4)
    def _(j):
        for half in range(2):
            load_rows(j, half).wait()
            for n in range(pieces):
                load(j, half, n).wait()
        group(j, 0)
        group(j, 1)

    edge_t[...] = edge[...].T
    e_copy.wait()
    first_lane = lax.broadcasted_iota(jnp.int32, (64, 128), 1) == 0

    def copy(q, n):
        at = q * 32 + n
        return pltpu.make_async_copy(
            yb.at[pl.ds(pl.multiple_of(at * 16, 16), 16)],
            out.at[pl.ds(pl.multiple_of(meta[1 + at] * 16, 16), 16)],
            sems.at[1],
        )

    @pl.loop(0, 2 * planes)
    def _(q):
        x = x_scr[q].reshape(512, 2 * BINS)

        def put(lag, y):
            for h in range(2):
                for c in range(CH_DEV):
                    part = y[c * 64 : c * 64 + 64, h * 128 : h * 128 + 128]
                    if lag + h == 0:
                        at = pl.ds(pl.multiple_of(q * 64, 64), 64)
                        part = jnp.where(first_lane, edge_t[at, c : c + 1], part)
                    yf[lag + h, pl.ds(c, 64, stride=8), :] = part
                at = pl.ds((lag + h) * 128, 128)
                yb[pl.ds(pl.multiple_of(q * 512, 512), 512), at] = yf[lag + h].astype(jnp.bfloat16)

        for n in range(2):
            lanes = pl.ds(n * 256, 256)
            even = jnp.dot(x[:, :BINS], e_scr[:BINS, lanes], preferred_element_type=jnp.float32)
            odd = jnp.dot(x[:, BINS:], e_scr[BINS:, lanes], preferred_element_type=jnp.float32)
            put(4 + 2 * n, even + odd)
            d_scr[:, lanes] = (even - odd).astype(jnp.bfloat16)
        put(2, jnp.dot(d_scr[...], flip[:, 256:], preferred_element_type=jnp.float32))
        put(0, jnp.dot(d_scr[:, 256:], flip[256:, :256], preferred_element_type=jnp.float32))

        @pl.loop(0, 32)
        def _(n):
            copy(q, n).start()

    pltpu.make_async_copy(yb, out.at[pl.ds(0, sources * CH_DEV)], sems.at[1]).wait()


def corr(meta, rows, mine, sib, inverse, out):
    first = out is None
    planes = sum(m.shape[0] for m in mine) // 128
    hbm = pl.BlockSpec(memory_space=pltpu.MemorySpace.HBM)
    args = [meta, rows, *mine, *sib, inverse] + ([] if first else [out])
    return pl.pallas_call(
        lambda *refs: corr_kernel(first, planes, len(mine), *refs),
        out_shape=jax.ShapeDtypeStruct((STEPS * 256 * CH_DEV, NLAG), jnp.bfloat16),
        in_specs=[pl.BlockSpec(memory_space=pltpu.SMEM)] + [hbm] * (len(args) - 1),
        out_specs=hbm,
        scratch_shapes=[
            pltpu.VMEM((2, 4, 32, GROUP), jnp.bfloat16),
            pltpu.VMEM((2, 4, 128 * planes, GROUP), jnp.bfloat16),
            pltpu.VMEM((2 * planes, CH_DEV, 64, 2 * BINS), jnp.bfloat16),
            pltpu.VMEM((2 * BINS, NLAG // 2), jnp.bfloat16),
            pltpu.VMEM((NLAG // 2, NLAG // 2), jnp.bfloat16),
            pltpu.VMEM((2, 16, 128, 128 * planes), jnp.bfloat16),
            pltpu.VMEM((128, 128 * planes), jnp.float32),
            pltpu.VMEM((128 * planes, 128), jnp.float32),
            pltpu.VMEM((512, NLAG // 2), jnp.bfloat16),
            pltpu.VMEM((8, 512, 128), jnp.float32),
            pltpu.VMEM((1024 * planes, NLAG), jnp.bfloat16),
            pltpu.SemaphoreType.DMA((2, 4)),
            pltpu.SemaphoreType.DMA((2,)),
        ],
        input_output_aliases={} if first else {3 + 2 * len(mine): 0},
        compiler_params=pltpu.CompilerParams(vmem_limit_bytes=60 * MIB),
        cost_estimate=pl.CostEstimate(
            flops=planes * 5 * 1024 * 2048 * 1024, bytes_accessed=12 * MIB, transcendentals=0
        ),
        name="corr",
    )(*args)


def device(x, y, z, core):
    return ((z // 2) * 2 + core) * 32 + (z % 2) * 16 + y * 4 + x


def line_pairs(axes, step):
    pairs = []
    for core in range(2):
        for n in range(64):
            at = {"x": n % 4, "y": n // 4 % 4, "z": n // 16}
            to = dict(at)
            to[axes[core]] = (at[axes[core]] + step) % 4
            pairs.append((device(**at, core=core), device(**to, core=core)))
    return pairs


CORE_PAIRS = [
    (device(n % 4, n // 4 % 4, n // 16, core), device(n % 4, n // 4 % 4, n // 16, 1 - core))
    for core in range(2)
    for n in range(64)
]


def line(block, axes):
    return [block] + [lax.ppermute(block, AXES, line_pairs(axes, s)) for s in (1, -1, 2)]


def local(records, channel_map, source_offset):
    forward, inverse = tables()
    forward, inverse = jnp.asarray(forward), jnp.asarray(inverse)
    grp, dev = lax.axis_index("grp"), lax.axis_index("dev")
    core = grp % 2
    x0, y0, z0 = dev % 4, dev // 4 % 4, (grp // 2) * 2 + dev // 16

    pick = (channel_map[0][:, None] == jnp.arange(256, dtype=jnp.int32)[None, :]).astype(jnp.bfloat16)
    ordered = jnp.dot(pick, records, preferred_element_type=jnp.float32).astype(jnp.bfloat16)
    regrouped = lax.all_to_all(ordered.reshape(32, 8, 512), "dev", split_axis=0, concat_axis=0, tiled=True)

    turns = (4 * core + 2 * jnp.arange(2, dtype=jnp.int32) - source_offset[:, 0]) % 8
    front_meta = jnp.stack([core, turns[0], turns[1]])
    white, keep, send = front(front_meta, regrouped.reshape(8, 4, 8, 512), forward)
    rows = channel_rows(white)
    block = keep + lax.ppermute(send, AXES, CORE_PAIRS)

    near = jnp.concatenate(line(block[None], "xz"), axis=0)
    off = jnp.array(OFFSETS, jnp.int32)
    outer, inner = jnp.meshgrid(off, off, indexing="ij")
    xs = (x0 + jnp.where(core == 0, inner, outer)) % 4
    zs = (z0 + jnp.where(core == 0, outer, inner)) % 4

    def places(offsets):
        ys = (y0 + jnp.array(offsets, jnp.int32).reshape(-1, 1, 1)) % 4
        chip = (zs // 2) * 64 + (zs % 2) * 16 + ys * 4 + xs
        place = chip.reshape(-1, 1, 1) + jnp.arange(2)[None, :, None] * 32 + jnp.arange(2)[None, None, :] * 128
        return jnp.concatenate([core[None], place.reshape(-1)]).astype(jnp.int32)

    def shift(x, step):
        return lax.ppermute(x, AXES, line_pairs("yy", step))

    def swap(xs):
        return [lax.ppermute(x, AXES, CORE_PAIRS) for x in xs]

    def flat(xs):
        return [x.reshape(-1, HALF) for x in xs]

    after = lax.optimization_barrier
    first = line(near, "zx")
    ahead, behind = shift(near, 1), shift(near, -1)
    near, ahead, *first = after((near, ahead, *first))
    second = line(ahead, "zx")
    across = shift(near, 2)
    behind_far = shift(first[3], -1)
    first_sib = swap(first)
    behind, across, *second = after((behind, across, *second))
    both = jnp.concatenate([behind, across], axis=0)
    rest = [both] + [lax.ppermute(both, AXES, line_pairs("zx", s)) for s in (1, -1)]
    across_far = lax.ppermute(across, AXES, line_pairs("zx", 2))
    second_sib = swap(second)
    out = corr(places((0, -1)), rows, flat(first + second), flat(first_sib + second_sib), inverse, None)
    out, *rest = after((out, *rest, behind_far, across_far))
    out = corr(places((1, 2)), rows, flat(rest), flat(swap(rest)), inverse, out)
    return out.reshape(1, STEPS * 256, CH_DEV, NLAG)


def solution(mesh):
    return jax.shard_map(
        local,
        mesh=mesh,
        in_specs=(P("grp", "dev"), P("grp", None), P(None, ("grp", "dev"))),
        out_specs=P(None, None, ("grp", "dev"), None),
        check_vma=False,
    )
```

```python
import math

import jax
import jax.numpy as jnp
import numpy as np
from jax import lax
from jax.experimental import pallas as pl
from jax.experimental.pallas import tpu as pltpu
from jax.sharding import PartitionSpec as P

W = 2048
BINS = 1024
NLAG = 1024
SEGS = 8
CH_DEV = 8
SRC_DEV = 2
STEPS = 2
KIN = 16
BLK = SEGS * 2 * KIN
NBLK = BINS // KIN
WIDE = NBLK * BLK
HALF = WIDE // 2
GROUP = 8 * BLK
AXES = ("grp", "dev")
MIB = 1 << 20
FACTOR = 2.0 / math.sqrt(SEGS * BINS)
OFFSETS = (0, -1, 1, 2)


def tables():
    turns = (np.arange(W)[:, None] * np.arange(BINS)[None, :]) % W
    angles = turns.astype(np.float32) * np.float32(2.0 * math.pi / W)
    forward = np.concatenate([np.cos(angles), -np.sin(angles)], axis=1)
    inv_turns = (np.arange(BINS)[:, None] * np.arange(NLAG // 2)[None, :]) % W
    inv_angles = inv_turns.astype(np.float32) * np.float32(2.0 * math.pi / W)
    inverse = np.concatenate([np.cos(inv_angles), -np.sin(inv_angles)], axis=0)
    return forward.astype(jnp.bfloat16), inverse.astype(jnp.bfloat16)


def chunk_transpose(vs):
    vs = list(vs)
    axis = vs[0].ndim - 1
    chunk = lax.broadcasted_iota(jnp.int32, vs[0].shape, axis) // 16
    for bit in (1, 2, 4):
        low = (chunk & bit) == 0
        for i in range(8):
            if i & bit == 0:
                a, b = vs[i], vs[i | bit]
                vs[i] = jnp.where(low, a, pltpu.roll(b, 16 * bit, axis))
                vs[i | bit] = jnp.where(low, pltpu.roll(a, 128 - 16 * bit, axis), b)
    return vs


def front_kernel(meta, rec, table_hbm, white, keep, send, spec, scr, table, sems):
    def load(n):
        rows = pl.ds(n * 256, 256)
        return pltpu.make_async_copy(table_hbm.at[rows], table.at[rows], sems.at[n])

    for n in range(8):
        load(n).start()
    total = None
    for q in range(4):
        x = rec[:, q].astype(jnp.float32).reshape(SEGS * CH_DEV, 512).astype(jnp.bfloat16)
        for h in range(2):
            n = 2 * q + h
            load(n).wait()
            part = jnp.dot(
                x[:, h * 256 : h * 256 + 256], table[n * 256 : n * 256 + 256, :], preferred_element_type=jnp.float32
            )
            total = part if total is None else total + part
    re, im = total[:, :BINS], total[:, BINS:]
    power = re * re + im * im
    water = jnp.sum(power, axis=1, keepdims=True) * (1.0 / BINS)
    wide = jnp.concatenate([power, jnp.zeros((SEGS * CH_DEV, 128), jnp.float32)], axis=1)
    run = wide
    for shift in (1, 2, 4):
        run = run + pltpu.roll(run, shift, 1)
    run = run + pltpu.roll(wide, 8, 1)
    smooth = pltpu.roll(run, BINS + 128 - 4, 1)[:, :BINS] * (1.0 / 9.0)
    scale = lax.rsqrt(smooth + water + 1e-5)
    spec[:, :BINS] = re * scale
    spec[:, BINS:] = im * scale
    for kv in range(8):
        for h in range(2):
            vs = [
                spec[g * 8 : g * 8 + 8, ri * BINS + kv * 128 : ri * BINS + kv * 128 + 128]
                for g in range(4 * h, 4 * h + 4)
                for ri in range(2)
            ]
            for j, w in enumerate(chunk_transpose(vs)):
                at = (kv * 8 + j) * BLK + h * 128
                scr[:, at : at + 128] = w
    white[...] = scr[...].astype(jnp.bfloat16)
    core = meta[0]
    pair = lax.broadcasted_iota(jnp.int32, (CH_DEV, HALF), 0) // 2
    for out, half in ((keep, core), (send, 1 - core)):
        x = scr[:, pl.ds(pl.multiple_of(half * HALF, HALF), HALF)]
        a = jnp.where(pair == 2 * core, pltpu.roll(x, meta[1], 0), 0.0)
        b = jnp.where(pair == 2 * core + 1, pltpu.roll(x, meta[2], 0), 0.0)
        out[...] = (a + b).astype(jnp.bfloat16)


def front(meta, rec, table):
    vmem = pl.BlockSpec(memory_space=pltpu.VMEM)
    return pl.pallas_call(
        front_kernel,
        out_shape=(
            jax.ShapeDtypeStruct((CH_DEV, WIDE), jnp.bfloat16),
            jax.ShapeDtypeStruct((CH_DEV, HALF), jnp.bfloat16),
            jax.ShapeDtypeStruct((CH_DEV, HALF), jnp.bfloat16),
        ),
        in_specs=[pl.BlockSpec(memory_space=pltpu.SMEM), vmem, pl.BlockSpec(memory_space=pltpu.MemorySpace.HBM)],
        out_specs=(vmem, vmem, vmem),
        scratch_shapes=[
            pltpu.VMEM((SEGS * CH_DEV, 2 * BINS), jnp.float32),
            pltpu.VMEM((CH_DEV, WIDE), jnp.float32),
            pltpu.VMEM((W, 2 * BINS), jnp.bfloat16),
            pltpu.SemaphoreType.DMA((8,)),
        ],
        compiler_params=pltpu.CompilerParams(vmem_limit_bytes=60 * MIB),
        name="front",
    )(meta, rec, table)


def rows_kernel(white, rows):
    own = white[...].astype(jnp.float32)
    lane = lax.broadcasted_iota(jnp.int32, (CH_DEV, WIDE), 1)
    turned = jnp.where(
        (lane & 16) == 0, -pltpu.roll(own, WIDE - 16, 1), pltpu.roll(own, 16, 1)
    )
    last = jnp.where((lane & 1) == 0, own, turned)
    last = jnp.where((lane & 2) == 0, last, -last)
    parts = [own, turned, last, jnp.zeros_like(own)]
    rows[...] = jnp.concatenate(parts, axis=0).astype(jnp.bfloat16)


def channel_rows(white):
    vmem = pl.BlockSpec(memory_space=pltpu.VMEM)
    return pl.pallas_call(
        rows_kernel,
        out_shape=jax.ShapeDtypeStruct((4 * CH_DEV, WIDE), jnp.bfloat16),
        in_specs=[vmem],
        out_specs=vmem,
        compiler_params=pltpu.CompilerParams(vmem_limit_bytes=16 * MIB),
        name="rows",
    )(white)


def corr_kernel(first, planes, arrays, meta, rows_hbm, *refs):
    pieces, sources = 4 * planes, 128 * planes
    mine, sib, e_hbm = refs[:arrays], refs[arrays : 2 * arrays], refs[2 * arrays]
    out, rows_scr, a_scr, x_scr, e_scr, flip, ov, edge, edge_t, d_scr, yf, yb, a_sems, sems = refs[2 * arrays + (1 if first else 2) :]

    def load(j, half, n):
        lines = (mine, sib)[half]
        if len(lines) == pieces:
            ref, row = lines[n], 0
        elif n % 4 < 3:
            ref, row = lines[n % 4], n // 4 * 32
        else:
            ref, row = lines[3 + n // 4], 0
        return pltpu.make_async_copy(
            ref.at[pl.ds(row, 32), pl.ds(pl.multiple_of(j * GROUP, GROUP), GROUP)],
            a_scr.at[half, j, pl.ds(n * 32, 32)],
            a_sems.at[half, j],
        )

    def load_rows(j, half):
        g = (core if half == 0 else 1 - core) * 4 + j
        return pltpu.make_async_copy(
            rows_hbm.at[:, pl.ds(pl.multiple_of(g * GROUP, GROUP), GROUP)],
            rows_scr.at[half, j],
            a_sems.at[half, j],
        )

    core = meta[0]
    for j in range(4):
        for half in range(2):
            load_rows(j, half).start()
            for n in range(pieces):
                load(j, half, n).start()
    e_copy = pltpu.make_async_copy(e_hbm, e_scr, sems.at[0])
    e_copy.start()
    diag = lax.broadcasted_iota(jnp.int32, (KIN, BLK), 0) == (
        lax.broadcasted_iota(jnp.int32, (KIN, BLK), 1) & 15
    )
    back = lax.broadcasted_iota(jnp.int32, (512, 512), 0) + lax.broadcasted_iota(jnp.int32, (512, 512), 1)
    flip[...] = jnp.where(back == 512, 1.0, 0.0).astype(jnp.bfloat16)
    edge[...] = jnp.zeros((128, sources), jnp.float32)

    def group(j, half):
        g = (core if half == 0 else 1 - core) * 4 + j
        for i in range(8):
            a = a_scr[half, j, :, i * BLK : i * BLK + BLK]
            if half == 1:
                a = jnp.concatenate(
                    [
                        a[128 * k + 32 * n + 8 * o : 128 * k + 32 * n + 8 * o + 8]
                        for k in range(planes)
                        for o in range(4)
                        for n in range(4)
                    ],
                    axis=0,
                )
            r = rows_scr[half, j, :, i * BLK : i * BLK + BLK].astype(jnp.float32)
            block = jnp.where(diag[None], r[:16, None, :], 0.0).astype(jnp.bfloat16)
            block = jnp.concatenate([block.reshape(256, BLK), r[16:].astype(jnp.bfloat16)], axis=0)
            prod = lax.dot_general(
                block, a, (((1,), (1,)), ((), ())), preferred_element_type=jnp.float32
            )
            prod = prod * FACTOR
            edge[0:8, :] += prod[256:264]
            ov[half, :, i * KIN : (i + 1) * KIN, :] = prod[:256].astype(jnp.bfloat16).reshape(16, KIN, sources)
        for ri in range(2):
            at = pl.ds(pl.multiple_of(ri * BINS + g * 128, 128), 128)
            for c in range(CH_DEV):
                x_scr[:, c, :, at] = ov[half, ri * 8 + c].T.reshape(2 * planes, 64, 128)

    @pl.loop(0, 4)
    def _(j):
        for half in range(2):
            load_rows(j, half).wait()
            for n in range(pieces):
                load(j, half, n).wait()
        group(j, 0)
        group(j, 1)

    edge_t[...] = edge[...].T
    e_copy.wait()
    first_lane = lax.broadcasted_iota(jnp.int32, (64, 128), 1) == 0

    def copy(q, n):
        at = q * 32 + n
        return pltpu.make_async_copy(
            yb.at[pl.ds(pl.multiple_of(at * 16, 16), 16)],
            out.at[pl.ds(pl.multiple_of(meta[1 + at] * 16, 16), 16)],
            sems.at[1],
        )

    for q in range(2 * planes):
        x = x_scr[q].reshape(512, 2 * BINS)

        def put(lag, y):
            for h in range(2):
                for c in range(CH_DEV):
                    part = y[c * 64 : c * 64 + 64, h * 128 : h * 128 + 128]
                    if lag + h == 0:
                        at = pl.ds(pl.multiple_of(q * 64, 64), 64)
                        part = jnp.where(first_lane, edge_t[at, c : c + 1], part)
                    yf[lag + h, pl.ds(c, 64, stride=8), :] = part
                at = pl.ds((lag + h) * 128, 128)
                yb[pl.ds(pl.multiple_of(q * 512, 512), 512), at] = yf[lag + h].astype(jnp.bfloat16)

        for n in range(2):
            lanes = pl.ds(n * 256, 256)
            even = jnp.dot(x[:, :BINS], e_scr[:BINS, lanes], preferred_element_type=jnp.float32)
            odd = jnp.dot(x[:, BINS:], e_scr[BINS:, lanes], preferred_element_type=jnp.float32)
            put(4 + 2 * n, even + odd)
            d_scr[:, lanes] = (even - odd).astype(jnp.bfloat16)
        put(2, jnp.dot(d_scr[...], flip[:, 256:], preferred_element_type=jnp.float32))
        put(0, jnp.dot(d_scr[:, 256:], flip[256:, :256], preferred_element_type=jnp.float32))

        for n in range(32):
            copy(q, n).start()

    pltpu.make_async_copy(yb, out.at[pl.ds(0, sources * CH_DEV)], sems.at[1]).wait()


def corr(meta, rows, mine, sib, inverse, out):
    first = out is None
    planes = sum(m.shape[0] for m in mine) // 128
    hbm = pl.BlockSpec(memory_space=pltpu.MemorySpace.HBM)
    args = [meta, rows, *mine, *sib, inverse] + ([] if first else [out])
    return pl.pallas_call(
        lambda *refs: corr_kernel(first, planes, len(mine), *refs),
        out_shape=jax.ShapeDtypeStruct((STEPS * 256 * CH_DEV, NLAG), jnp.bfloat16),
        in_specs=[pl.BlockSpec(memory_space=pltpu.SMEM)] + [hbm] * (len(args) - 1),
        out_specs=hbm,
        scratch_shapes=[
            pltpu.VMEM((2, 4, 32, GROUP), jnp.bfloat16),
            pltpu.VMEM((2, 4, 128 * planes, GROUP), jnp.bfloat16),
            pltpu.VMEM((2 * planes, CH_DEV, 64, 2 * BINS), jnp.bfloat16),
            pltpu.VMEM((2 * BINS, NLAG // 2), jnp.bfloat16),
            pltpu.VMEM((NLAG // 2, NLAG // 2), jnp.bfloat16),
            pltpu.VMEM((2, 16, 128, 128 * planes), jnp.bfloat16),
            pltpu.VMEM((128, 128 * planes), jnp.float32),
            pltpu.VMEM((128 * planes, 128), jnp.float32),
            pltpu.VMEM((512, NLAG // 2), jnp.bfloat16),
            pltpu.VMEM((8, 512, 128), jnp.float32),
            pltpu.VMEM((1024 * planes, NLAG), jnp.bfloat16),
            pltpu.SemaphoreType.DMA((2, 4)),
            pltpu.SemaphoreType.DMA((2,)),
        ],
        input_output_aliases={} if first else {3 + 2 * len(mine): 0},
        compiler_params=pltpu.CompilerParams(vmem_limit_bytes=60 * MIB),
        cost_estimate=pl.CostEstimate(
            flops=planes * 5 * 1024 * 2048 * 1024, bytes_accessed=12 * MIB, transcendentals=0
        ),
        name="corr",
    )(*args)


def device(x, y, z, core):
    return ((z // 2) * 2 + core) * 32 + (z % 2) * 16 + y * 4 + x


def line_pairs(axes, step):
    pairs = []
    for core in range(2):
        for n in range(64):
            at = {"x": n % 4, "y": n // 4 % 4, "z": n // 16}
            to = dict(at)
            to[axes[core]] = (at[axes[core]] + step) % 4
            pairs.append((device(**at, core=core), device(**to, core=core)))
    return pairs


CORE_PAIRS = [
    (device(n % 4, n // 4 % 4, n // 16, core), device(n % 4, n // 4 % 4, n // 16, 1 - core))
    for core in range(2)
    for n in range(64)
]


def line(block, axes):
    return [block] + [lax.ppermute(block, AXES, line_pairs(axes, s)) for s in (1, -1, 2)]


def local(records, channel_map, source_offset):
    forward, inverse = tables()
    forward, inverse = jnp.asarray(forward), jnp.asarray(inverse)
    grp, dev = lax.axis_index("grp"), lax.axis_index("dev")
    core = grp % 2
    x0, y0, z0 = dev % 4, dev // 4 % 4, (grp // 2) * 2 + dev // 16

    pick = (channel_map[0][:, None] == jnp.arange(256, dtype=jnp.int32)[None, :]).astype(jnp.bfloat16)
    ordered = jnp.dot(pick, records, preferred_element_type=jnp.float32).astype(jnp.bfloat16)
    regrouped = lax.all_to_all(ordered.reshape(32, 8, 512), "dev", split_axis=0, concat_axis=0, tiled=True)

    turns = (4 * core + 2 * jnp.arange(2, dtype=jnp.int32) - source_offset[:, 0]) % 8
    front_meta = jnp.stack([core, turns[0], turns[1]])
    white, keep, send = front(front_meta, regrouped.reshape(8, 4, 8, 512), forward)
    rows = channel_rows(white)
    block = keep + lax.ppermute(send, AXES, CORE_PAIRS)

    near = jnp.concatenate(line(block[None], "xz"), axis=0)
    off = jnp.array(OFFSETS, jnp.int32)
    outer, inner = jnp.meshgrid(off, off, indexing="ij")
    xs = (x0 + jnp.where(core == 0, inner, outer)) % 4
    zs = (z0 + jnp.where(core == 0, outer, inner)) % 4

    def places(offsets):
        ys = (y0 + jnp.array(offsets, jnp.int32).reshape(-1, 1, 1)) % 4
        chip = (zs // 2) * 64 + (zs % 2) * 16 + ys * 4 + xs
        place = chip.reshape(-1, 1, 1) + jnp.arange(2)[None, :, None] * 32 + jnp.arange(2)[None, None, :] * 128
        return jnp.concatenate([core[None], place.reshape(-1)]).astype(jnp.int32)

    def shift(x, step):
        return lax.ppermute(x, AXES, line_pairs("yy", step))

    def swap(xs):
        return [lax.ppermute(x, AXES, CORE_PAIRS) for x in xs]

    def flat(xs):
        return [x.reshape(-1, HALF) for x in xs]

    after = lax.optimization_barrier
    first = line(near, "zx")
    ahead, behind = shift(near, 1), shift(near, -1)
    near, ahead, *first = after((near, ahead, *first))
    second = line(ahead, "zx")
    across = shift(near, 2)
    behind_far = shift(first[3], -1)
    first_sib = swap(first)
    behind, across, *second = after((behind, across, *second))
    both = jnp.concatenate([behind, across], axis=0)
    rest = [both] + [lax.ppermute(both, AXES, line_pairs("zx", s)) for s in (1, -1)]
    across_far = lax.ppermute(across, AXES, line_pairs("zx", 2))
    second_sib = swap(second)
    both_sib = swap([both, behind_far])
    out = corr(places((0, -1)), rows, flat(first + second), flat(first_sib + second_sib), inverse, None)
    out, *rest = after((out, *rest, behind_far, across_far))
    far = swap([rest[1], rest[2], rest[4]])
    rest_sib = [both_sib[0], far[0], far[1], both_sib[1], far[2]]
    out = corr(places((1, 2)), rows, flat(rest), flat(rest_sib), inverse, out)
    return out.reshape(1, STEPS * 256, CH_DEV, NLAG)


def solution(mesh):
    return jax.shard_map(
        local,
        mesh=mesh,
        in_specs=(P("grp", "dev"), P("grp", None), P(None, ("grp", "dev"))),
        out_specs=P(None, None, ("grp", "dev"), None),
        check_vma=False,
    )
```

```python
import math

import jax
import jax.numpy as jnp
import numpy as np
from jax import lax
from jax.experimental import pallas as pl
from jax.experimental.pallas import tpu as pltpu
from jax.sharding import PartitionSpec as P

W = 2048
BINS = 1024
NLAG = 1024
SEGS = 8
CH_DEV = 8
SRC_DEV = 2
STEPS = 2
KIN = 16
BLK = SEGS * 2 * KIN
NBLK = BINS // KIN
WIDE = NBLK * BLK
HALF = WIDE // 2
GROUP = 8 * BLK
AXES = ("grp", "dev")
MIB = 1 << 20
FACTOR = 2.0 / math.sqrt(SEGS * BINS)
OFFSETS = (0, -1, 1, 2)


def tables():
    turns = (np.arange(W)[:, None] * np.arange(BINS)[None, :]) % W
    angles = turns.astype(np.float32) * np.float32(2.0 * math.pi / W)
    forward = np.concatenate([np.cos(angles), -np.sin(angles)], axis=1)
    inv_turns = (np.arange(BINS)[:, None] * np.arange(NLAG // 2)[None, :]) % W
    inv_angles = inv_turns.astype(np.float32) * np.float32(2.0 * math.pi / W)
    inverse = np.concatenate([np.cos(inv_angles), -np.sin(inv_angles)], axis=0)
    return forward.astype(jnp.bfloat16), inverse.astype(jnp.bfloat16)


def chunk_transpose(vs):
    vs = list(vs)
    axis = vs[0].ndim - 1
    chunk = lax.broadcasted_iota(jnp.int32, vs[0].shape, axis) // 16
    for bit in (1, 2, 4):
        low = (chunk & bit) == 0
        for i in range(8):
            if i & bit == 0:
                a, b = vs[i], vs[i | bit]
                vs[i] = jnp.where(low, a, pltpu.roll(b, 16 * bit, axis))
                vs[i | bit] = jnp.where(low, pltpu.roll(a, 128 - 16 * bit, axis), b)
    return vs


def front_kernel(meta, rec, table, white, keep, send, spec, scr):
    total = None
    for q in range(4):
        x = rec[:, q].astype(jnp.float32).reshape(SEGS * CH_DEV, 512).astype(jnp.bfloat16)
        part = jnp.dot(x, table[q * 512 : (q + 1) * 512, :], preferred_element_type=jnp.float32)
        total = part if total is None else total + part
    re, im = total[:, :BINS], total[:, BINS:]
    power = re * re + im * im
    water = jnp.sum(power, axis=1, keepdims=True) * (1.0 / BINS)
    wide = jnp.concatenate([power, jnp.zeros((SEGS * CH_DEV, 128), jnp.float32)], axis=1)
    run = wide
    for shift in (1, 2, 4):
        run = run + pltpu.roll(run, shift, 1)
    run = run + pltpu.roll(wide, 8, 1)
    smooth = pltpu.roll(run, BINS + 128 - 4, 1)[:, :BINS] * (1.0 / 9.0)
    scale = lax.rsqrt(smooth + water + 1e-5)
    spec[:, :BINS] = re * scale
    spec[:, BINS:] = im * scale
    for kv in range(8):
        for h in range(2):
            vs = [
                spec[g * 8 : g * 8 + 8, ri * BINS + kv * 128 : ri * BINS + kv * 128 + 128]
                for g in range(4 * h, 4 * h + 4)
                for ri in range(2)
            ]
            for j, w in enumerate(chunk_transpose(vs)):
                at = (kv * 8 + j) * BLK + h * 128
                scr[:, at : at + 128] = w
    white[...] = scr[...].astype(jnp.bfloat16)
    core = meta[0]
    pair = lax.broadcasted_iota(jnp.int32, (CH_DEV, HALF), 0) // 2
    for out, half in ((keep, core), (send, 1 - core)):
        x = scr[:, pl.ds(pl.multiple_of(half * HALF, HALF), HALF)]
        a = jnp.where(pair == 2 * core, pltpu.roll(x, meta[1], 0), 0.0)
        b = jnp.where(pair == 2 * core + 1, pltpu.roll(x, meta[2], 0), 0.0)
        out[...] = (a + b).astype(jnp.bfloat16)


def front(meta, rec, table):
    vmem = pl.BlockSpec(memory_space=pltpu.VMEM)
    return pl.pallas_call(
        front_kernel,
        out_shape=(
            jax.ShapeDtypeStruct((CH_DEV, WIDE), jnp.bfloat16),
            jax.ShapeDtypeStruct((CH_DEV, HALF), jnp.bfloat16),
            jax.ShapeDtypeStruct((CH_DEV, HALF), jnp.bfloat16),
        ),
        in_specs=[pl.BlockSpec(memory_space=pltpu.SMEM), vmem, vmem],
        out_specs=(vmem, vmem, vmem),
        scratch_shapes=[
            pltpu.VMEM((SEGS * CH_DEV, 2 * BINS), jnp.float32),
            pltpu.VMEM((CH_DEV, WIDE), jnp.float32),
        ],
        compiler_params=pltpu.CompilerParams(vmem_limit_bytes=32 * MIB),
        name="front",
    )(meta, rec, table)


def rows_kernel(white, rows):
    own = white[...].astype(jnp.float32)
    lane = lax.broadcasted_iota(jnp.int32, (CH_DEV, WIDE), 1)
    turned = jnp.where(
        (lane & 16) == 0, -pltpu.roll(own, WIDE - 16, 1), pltpu.roll(own, 16, 1)
    )
    last = jnp.where((lane & 1) == 0, own, turned)
    last = jnp.where((lane & 2) == 0, last, -last)
    parts = [own, turned, last, jnp.zeros_like(own)]
    rows[...] = jnp.concatenate(parts, axis=0).astype(jnp.bfloat16)


def channel_rows(white):
    vmem = pl.BlockSpec(memory_space=pltpu.VMEM)
    return pl.pallas_call(
        rows_kernel,
        out_shape=jax.ShapeDtypeStruct((4 * CH_DEV, WIDE), jnp.bfloat16),
        in_specs=[vmem],
        out_specs=vmem,
        compiler_params=pltpu.CompilerParams(vmem_limit_bytes=16 * MIB),
        name="rows",
    )(white)


def corr_kernel(first, planes, arrays, meta, rows_hbm, *refs):
    pieces, sources = 4 * planes, 128 * planes
    mine, sib, e_hbm = refs[:arrays], refs[arrays : 2 * arrays], refs[2 * arrays]
    out, rows_scr, a_scr, x_scr, e_scr, flip, ov, edge, edge_t, d_scr, yf, yb, a_sems, sems = refs[2 * arrays + (1 if first else 2) :]

    def load(j, half, n):
        lines = (mine, sib)[half]
        if len(lines) == pieces:
            ref, row = lines[n], 0
        elif n % 4 < 3:
            ref, row = lines[n % 4], n // 4 * 32
        else:
            ref, row = lines[3 + n // 4], 0
        return pltpu.make_async_copy(
            ref.at[pl.ds(row, 32), pl.ds(pl.multiple_of(j * GROUP, GROUP), GROUP)],
            a_scr.at[half, j, pl.ds(n * 32, 32)],
            a_sems.at[half, j],
        )

    def load_rows(j, half):
        g = (core if half == 0 else 1 - core) * 4 + j
        return pltpu.make_async_copy(
            rows_hbm.at[:, pl.ds(pl.multiple_of(g * GROUP, GROUP), GROUP)],
            rows_scr.at[half, j],
            a_sems.at[half, j],
        )

    core = meta[0]
    for j in range(4):
        for half in range(2):
            load_rows(j, half).start()
            for n in range(pieces):
                load(j, half, n).start()
    e_copy = pltpu.make_async_copy(e_hbm, e_scr, sems.at[0])
    e_copy.start()
    diag = lax.broadcasted_iota(jnp.int32, (KIN, BLK), 0) == (
        lax.broadcasted_iota(jnp.int32, (KIN, BLK), 1) & 15
    )
    back = lax.broadcasted_iota(jnp.int32, (512, 512), 0) + lax.broadcasted_iota(jnp.int32, (512, 512), 1)
    flip[...] = jnp.where(back == 512, 1.0, 0.0).astype(jnp.bfloat16)
    edge[...] = jnp.zeros((128, sources), jnp.float32)

    def group(j, half):
        g = (core if half == 0 else 1 - core) * 4 + j
        for i in range(8):
            a = a_scr[half, j, :, i * BLK : i * BLK + BLK]
            if half == 1:
                a = jnp.concatenate(
                    [
                        a[128 * k + 32 * n + 8 * o : 128 * k + 32 * n + 8 * o + 8]
                        for k in range(planes)
                        for o in range(4)
                        for n in range(4)
                    ],
                    axis=0,
                )
            r = rows_scr[half, j, :, i * BLK : i * BLK + BLK].astype(jnp.float32)
            block = jnp.where(diag[None], r[:16, None, :], 0.0).astype(jnp.bfloat16)
            block = jnp.concatenate([block.reshape(256, BLK), r[16:].astype(jnp.bfloat16)], axis=0)
            prod = lax.dot_general(
                block, a, (((1,), (1,)), ((), ())), preferred_element_type=jnp.float32
            )
            prod = prod * FACTOR
            edge[0:8, :] += prod[256:264]
            ov[half, :, i * KIN : (i + 1) * KIN, :] = prod[:256].astype(jnp.bfloat16).reshape(16, KIN, sources)
        for ri in range(2):
            at = pl.ds(pl.multiple_of(ri * BINS + g * 128, 128), 128)
            for c in range(CH_DEV):
                x_scr[:, c, :, at] = ov[half, ri * 8 + c].T.reshape(2 * planes, 64, 128)

    @pl.loop(0, 4)
    def _(j):
        for half in range(2):
            load_rows(j, half).wait()
            for n in range(pieces):
                load(j, half, n).wait()
        group(j, 0)
        group(j, 1)

    edge_t[...] = edge[...].T
    e_copy.wait()
    first_lane = lax.broadcasted_iota(jnp.int32, (64, 128), 1) == 0

    def copy(q, n):
        at = q * 32 + n
        return pltpu.make_async_copy(
            yb.at[pl.ds(pl.multiple_of(at * 16, 16), 16)],
            out.at[pl.ds(pl.multiple_of(meta[1 + at] * 16, 16), 16)],
            sems.at[1],
        )

    for q in range(2 * planes):
        x = x_scr[q].reshape(512, 2 * BINS)

        def put(lag, y):
            for h in range(2):
                for c in range(CH_DEV):
                    part = y[c * 64 : c * 64 + 64, h * 128 : h * 128 + 128]
                    if lag + h == 0:
                        at = pl.ds(pl.multiple_of(q * 64, 64), 64)
                        part = jnp.where(first_lane, edge_t[at, c : c + 1], part)
                    yf[lag + h, pl.ds(c, 64, stride=8), :] = part
                at = pl.ds((lag + h) * 128, 128)
                yb[pl.ds(pl.multiple_of(q * 512, 512), 512), at] = yf[lag + h].astype(jnp.bfloat16)

        for n in range(2):
            lanes = pl.ds(n * 256, 256)
            even = jnp.dot(x[:, :BINS], e_scr[:BINS, lanes], preferred_element_type=jnp.float32)
            odd = jnp.dot(x[:, BINS:], e_scr[BINS:, lanes], preferred_element_type=jnp.float32)
            put(4 + 2 * n, even + odd)
            d_scr[:, lanes] = (even - odd).astype(jnp.bfloat16)
        put(2, jnp.dot(d_scr[...], flip[:, 256:], preferred_element_type=jnp.float32))
        put(0, jnp.dot(d_scr[:, 256:], flip[256:, :256], preferred_element_type=jnp.float32))

        for n in range(32):
            copy(q, n).start()

    pltpu.make_async_copy(yb, out.at[pl.ds(0, sources * CH_DEV)], sems.at[1]).wait()


def corr(meta, rows, mine, sib, inverse, out):
    first = out is None
    planes = sum(m.shape[0] for m in mine) // 128
    hbm = pl.BlockSpec(memory_space=pltpu.MemorySpace.HBM)
    args = [meta, rows, *mine, *sib, inverse] + ([] if first else [out])
    return pl.pallas_call(
        lambda *refs: corr_kernel(first, planes, len(mine), *refs),
        out_shape=jax.ShapeDtypeStruct((STEPS * 256 * CH_DEV, NLAG), jnp.bfloat16),
        in_specs=[pl.BlockSpec(memory_space=pltpu.SMEM)] + [hbm] * (len(args) - 1),
        out_specs=hbm,
        scratch_shapes=[
            pltpu.VMEM((2, 4, 32, GROUP), jnp.bfloat16),
            pltpu.VMEM((2, 4, 128 * planes, GROUP), jnp.bfloat16),
            pltpu.VMEM((2 * planes, CH_DEV, 64, 2 * BINS), jnp.bfloat16),
            pltpu.VMEM((2 * BINS, NLAG // 2), jnp.bfloat16),
            pltpu.VMEM((NLAG // 2, NLAG // 2), jnp.bfloat16),
            pltpu.VMEM((2, 16, 128, 128 * planes), jnp.bfloat16),
            pltpu.VMEM((128, 128 * planes), jnp.float32),
            pltpu.VMEM((128 * planes, 128), jnp.float32),
            pltpu.VMEM((512, NLAG // 2), jnp.bfloat16),
            pltpu.VMEM((8, 512, 128), jnp.float32),
            pltpu.VMEM((1024 * planes, NLAG), jnp.bfloat16),
            pltpu.SemaphoreType.DMA((2, 4)),
            pltpu.SemaphoreType.DMA((2,)),
        ],
        input_output_aliases={} if first else {3 + 2 * len(mine): 0},
        compiler_params=pltpu.CompilerParams(vmem_limit_bytes=60 * MIB),
        cost_estimate=pl.CostEstimate(
            flops=planes * 5 * 1024 * 2048 * 1024, bytes_accessed=12 * MIB, transcendentals=0
        ),
        name="corr",
    )(*args)


def device(x, y, z, core):
    return ((z // 2) * 2 + core) * 32 + (z % 2) * 16 + y * 4 + x


def line_pairs(axes, step):
    pairs = []
    for core in range(2):
        for n in range(64):
            at = {"x": n % 4, "y": n // 4 % 4, "z": n // 16}
            to = dict(at)
            to[axes[core]] = (at[axes[core]] + step) % 4
            pairs.append((device(**at, core=core), device(**to, core=core)))
    return pairs


CORE_PAIRS = [
    (device(n % 4, n // 4 % 4, n // 16, core), device(n % 4, n // 4 % 4, n // 16, 1 - core))
    for core in range(2)
    for n in range(64)
]


def line(block, axes):
    return [block] + [lax.ppermute(block, AXES, line_pairs(axes, s)) for s in (1, -1, 2)]


def local(records, channel_map, source_offset):
    forward, inverse = tables()
    forward, inverse = jnp.asarray(forward), jnp.asarray(inverse)
    grp, dev = lax.axis_index("grp"), lax.axis_index("dev")
    core = grp % 2
    x0, y0, z0 = dev % 4, dev // 4 % 4, (grp // 2) * 2 + dev // 16

    pick = (channel_map[0][:, None] == jnp.arange(256, dtype=jnp.int32)[None, :]).astype(jnp.bfloat16)
    pick = lax.optimization_barrier(pick)
    ordered = jnp.dot(pick, records, preferred_element_type=jnp.float32).astype(jnp.bfloat16)
    regrouped = lax.all_to_all(ordered.reshape(32, 8, 512), "dev", split_axis=0, concat_axis=0, tiled=True)

    turns = (4 * core + 2 * jnp.arange(2, dtype=jnp.int32) - source_offset[:, 0]) % 8
    front_meta = jnp.stack([core, turns[0], turns[1]])
    white, keep, send = front(front_meta, regrouped.reshape(8, 4, 8, 512), forward)
    rows = channel_rows(white)
    block = keep + lax.ppermute(send, AXES, CORE_PAIRS)

    near = jnp.concatenate(line(block[None], "xz"), axis=0)
    off = jnp.array(OFFSETS, jnp.int32)
    outer, inner = jnp.meshgrid(off, off, indexing="ij")
    xs = (x0 + jnp.where(core == 0, inner, outer)) % 4
    zs = (z0 + jnp.where(core == 0, outer, inner)) % 4

    def places(offsets):
        ys = (y0 + jnp.array(offsets, jnp.int32).reshape(-1, 1, 1)) % 4
        chip = (zs // 2) * 64 + (zs % 2) * 16 + ys * 4 + xs
        place = chip.reshape(-1, 1, 1) + jnp.arange(2)[None, :, None] * 32 + jnp.arange(2)[None, None, :] * 128
        return jnp.concatenate([core[None], place.reshape(-1)]).astype(jnp.int32)

    def shift(x, step):
        return lax.ppermute(x, AXES, line_pairs("yy", step))

    def swap(xs):
        return [lax.ppermute(x, AXES, CORE_PAIRS) for x in xs]

    def flat(xs):
        return [x.reshape(-1, HALF) for x in xs]

    after = lax.optimization_barrier
    first = line(near, "zx")
    ahead, behind = shift(near, 1), shift(near, -1)
    near, ahead, *first = after((near, ahead, *first))
    second = line(ahead, "zx")
    across = shift(near, 2)
    behind_far = shift(first[3], -1)
    first_sib = swap(first)
    behind, across, *second = after((behind, across, *second))
    both = jnp.concatenate([behind, across], axis=0)
    rest = [both] + [lax.ppermute(both, AXES, line_pairs("zx", s)) for s in (1, -1)]
    across_far = lax.ppermute(across, AXES, line_pairs("zx", 2))
    second_sib = swap(second)
    both_sib = swap([both, behind_far])
    out = corr(places((0, -1)), rows, flat(first + second), flat(first_sib + second_sib), inverse, None)
    out, *rest = after((out, *rest, behind_far, across_far))
    far = swap([rest[1], rest[2], rest[4]])
    rest_sib = [both_sib[0], far[0], far[1], both_sib[1], far[2]]
    out = corr(places((1, 2)), rows, flat(rest), flat(rest_sib), inverse, out)
    return out.reshape(1, STEPS * 256, CH_DEV, NLAG)


def solution(mesh):
    return jax.shard_map(
        local,
        mesh=mesh,
        in_specs=(P("grp", "dev"), P("grp", None), P(None, ("grp", "dev"))),
        out_specs=P(None, None, ("grp", "dev"), None),
        check_vma=False,
    )
```

```python
import math

import jax
import jax.numpy as jnp
import numpy as np
from jax import lax
from jax.experimental import pallas as pl
from jax.experimental.pallas import tpu as pltpu
from jax.sharding import PartitionSpec as P

W = 2048
BINS = 1024
NLAG = 1024
SEGS = 8
CH_DEV = 8
SRC_DEV = 2
STEPS = 2
KIN = 16
BLK = SEGS * 2 * KIN
NBLK = BINS // KIN
WIDE = NBLK * BLK
HALF = WIDE // 2
GROUP = 8 * BLK
AXES = ("grp", "dev")
MIB = 1 << 20
FACTOR = 2.0 / math.sqrt(SEGS * BINS)
OFFSETS = (0, -1, 1, 2)


def tables():
    turns = (np.arange(W)[:, None] * np.arange(BINS)[None, :]) % W
    angles = turns.astype(np.float32) * np.float32(2.0 * math.pi / W)
    forward = np.concatenate([np.cos(angles), -np.sin(angles)], axis=1)
    inv_turns = (np.arange(BINS)[:, None] * np.arange(NLAG // 2)[None, :]) % W
    inv_angles = inv_turns.astype(np.float32) * np.float32(2.0 * math.pi / W)
    inverse = np.concatenate([np.cos(inv_angles), -np.sin(inv_angles)], axis=0)
    return forward.astype(jnp.bfloat16), inverse.astype(jnp.bfloat16)


def chunk_transpose(vs):
    vs = list(vs)
    axis = vs[0].ndim - 1
    chunk = lax.broadcasted_iota(jnp.int32, vs[0].shape, axis) // 16
    for bit in (1, 2, 4):
        low = (chunk & bit) == 0
        for i in range(8):
            if i & bit == 0:
                a, b = vs[i], vs[i | bit]
                vs[i] = jnp.where(low, a, pltpu.roll(b, 16 * bit, axis))
                vs[i | bit] = jnp.where(low, pltpu.roll(a, 128 - 16 * bit, axis), b)
    return vs


def front_kernel(meta, rec, table, white, keep, send, spec, scr):
    total = None
    for q in range(4):
        x = rec[:, q].astype(jnp.float32).reshape(SEGS * CH_DEV, 512).astype(jnp.bfloat16)
        part = jnp.dot(x, table[q * 512 : (q + 1) * 512, :], preferred_element_type=jnp.float32)
        total = part if total is None else total + part
    re, im = total[:, :BINS], total[:, BINS:]
    power = re * re + im * im
    water = jnp.sum(power, axis=1, keepdims=True) * (1.0 / BINS)
    wide = jnp.concatenate([power, jnp.zeros((SEGS * CH_DEV, 128), jnp.float32)], axis=1)
    run = wide
    for shift in (1, 2, 4):
        run = run + pltpu.roll(run, shift, 1)
    run = run + pltpu.roll(wide, 8, 1)
    smooth = pltpu.roll(run, BINS + 128 - 4, 1)[:, :BINS] * (1.0 / 9.0)
    scale = lax.rsqrt(smooth + water + 1e-5)
    spec[:, :BINS] = re * scale
    spec[:, BINS:] = im * scale
    for kv in range(8):
        for h in range(2):
            vs = [
                spec[g * 8 : g * 8 + 8, ri * BINS + kv * 128 : ri * BINS + kv * 128 + 128]
                for g in range(4 * h, 4 * h + 4)
                for ri in range(2)
            ]
            for j, w in enumerate(chunk_transpose(vs)):
                at = (kv * 8 + j) * BLK + h * 128
                scr[:, at : at + 128] = w
    white[...] = scr[...].astype(jnp.bfloat16)
    core = meta[0]
    pair = lax.broadcasted_iota(jnp.int32, (CH_DEV, HALF), 0) // 2
    for out, half in ((keep, core), (send, 1 - core)):
        x = scr[:, pl.ds(pl.multiple_of(half * HALF, HALF), HALF)]
        a = jnp.where(pair == 2 * core, pltpu.roll(x, meta[1], 0), 0.0)
        b = jnp.where(pair == 2 * core + 1, pltpu.roll(x, meta[2], 0), 0.0)
        out[...] = (a + b).astype(jnp.bfloat16)


def front(meta, rec, table):
    vmem = pl.BlockSpec(memory_space=pltpu.VMEM)
    return pl.pallas_call(
        front_kernel,
        out_shape=(
            jax.ShapeDtypeStruct((CH_DEV, WIDE), jnp.bfloat16),
            jax.ShapeDtypeStruct((CH_DEV, HALF), jnp.bfloat16),
            jax.ShapeDtypeStruct((CH_DEV, HALF), jnp.bfloat16),
        ),
        in_specs=[pl.BlockSpec(memory_space=pltpu.SMEM), vmem, vmem],
        out_specs=(vmem, vmem, vmem),
        scratch_shapes=[
            pltpu.VMEM((SEGS * CH_DEV, 2 * BINS), jnp.float32),
            pltpu.VMEM((CH_DEV, WIDE), jnp.float32),
        ],
        compiler_params=pltpu.CompilerParams(vmem_limit_bytes=32 * MIB),
        name="front",
    )(meta, rec, table)


def rows_kernel(white, rows):
    own = white[...].astype(jnp.float32)
    lane = lax.broadcasted_iota(jnp.int32, (CH_DEV, WIDE), 1)
    turned = jnp.where(
        (lane & 16) == 0, -pltpu.roll(own, WIDE - 16, 1), pltpu.roll(own, 16, 1)
    )
    last = jnp.where((lane & 1) == 0, own, turned)
    last = jnp.where((lane & 2) == 0, last, -last)
    parts = [own, turned, last, jnp.zeros_like(own)]
    rows[...] = jnp.concatenate(parts, axis=0).astype(jnp.bfloat16)


def channel_rows(white):
    vmem = pl.BlockSpec(memory_space=pltpu.VMEM)
    return pl.pallas_call(
        rows_kernel,
        out_shape=jax.ShapeDtypeStruct((4 * CH_DEV, WIDE), jnp.bfloat16),
        in_specs=[vmem],
        out_specs=vmem,
        compiler_params=pltpu.CompilerParams(vmem_limit_bytes=16 * MIB),
        name="rows",
    )(white)


def corr_kernel(first, planes, arrays, meta, rows_hbm, *refs):
    pieces, sources = 4 * planes, 128 * planes
    mine, sib, e_hbm = refs[:arrays], refs[arrays : 2 * arrays], refs[2 * arrays]
    out, rows_scr, a_scr, x_scr, e_scr, flip, ov, edge, edge_t, d_scr, yf, yb, a_sems, sems = refs[2 * arrays + (1 if first else 2) :]

    def load(j, half, n):
        lines = (mine, sib)[half]
        if len(lines) == pieces:
            ref, row = lines[n], 0
        elif n % 4 < 3:
            ref, row = lines[n % 4], n // 4 * 32
        else:
            ref, row = lines[3 + n // 4], 0
        return pltpu.make_async_copy(
            ref.at[pl.ds(row, 32), pl.ds(pl.multiple_of(j * GROUP, GROUP), GROUP)],
            a_scr.at[half, j, pl.ds(n * 32, 32)],
            a_sems.at[half, j],
        )

    def load_rows(j, half):
        g = (core if half == 0 else 1 - core) * 4 + j
        return pltpu.make_async_copy(
            rows_hbm.at[:, pl.ds(pl.multiple_of(g * GROUP, GROUP), GROUP)],
            rows_scr.at[half, j],
            a_sems.at[half, j],
        )

    core = meta[0]
    for j in range(4):
        for half in range(2):
            load_rows(j, half).start()
            for n in range(pieces):
                load(j, half, n).start()
    e_copy = pltpu.make_async_copy(e_hbm, e_scr, sems.at[0])
    e_copy.start()
    diag = lax.broadcasted_iota(jnp.int32, (KIN, BLK), 0) == (
        lax.broadcasted_iota(jnp.int32, (KIN, BLK), 1) & 15
    )
    back = lax.broadcasted_iota(jnp.int32, (512, 512), 0) + lax.broadcasted_iota(jnp.int32, (512, 512), 1)
    flip[...] = jnp.where(back == 512, 1.0, 0.0).astype(jnp.bfloat16)
    edge[...] = jnp.zeros((128, sources), jnp.float32)

    def group(j, half):
        g = (core if half == 0 else 1 - core) * 4 + j
        for i in range(8):
            a = a_scr[half, j, :, i * BLK : i * BLK + BLK]
            if half == 1:
                a = jnp.concatenate(
                    [
                        a[128 * k + 32 * n + 8 * o : 128 * k + 32 * n + 8 * o + 8]
                        for k in range(planes)
                        for o in range(4)
                        for n in range(4)
                    ],
                    axis=0,
                )
            r = rows_scr[half, j, :, i * BLK : i * BLK + BLK].astype(jnp.float32)
            block = jnp.where(diag[None], r[:16, None, :], 0.0).astype(jnp.bfloat16)
            block = jnp.concatenate([block.reshape(256, BLK), r[16:].astype(jnp.bfloat16)], axis=0)
            prod = lax.dot_general(
                block, a, (((1,), (1,)), ((), ())), preferred_element_type=jnp.float32
            )
            prod = prod * FACTOR
            edge[0:8, :] += prod[256:264]
            ov[half, :, i * KIN : (i + 1) * KIN, :] = prod[:256].astype(jnp.bfloat16).reshape(16, KIN, sources)
        for ri in range(2):
            at = pl.ds(pl.multiple_of(ri * BINS + g * 128, 128), 128)
            for c in range(CH_DEV):
                x_scr[:, c, :, at] = ov[half, ri * 8 + c].T.reshape(2 * planes, 64, 128)

    @pl.loop(0, 4)
    def _(j):
        for half in range(2):
            load_rows(j, half).wait()
            for n in range(pieces):
                load(j, half, n).wait()
        group(j, 0)
        group(j, 1)

    edge_t[...] = edge[...].T
    e_copy.wait()
    first_lane = lax.broadcasted_iota(jnp.int32, (64, 128), 1) == 0

    def copy(q, n):
        at = q * 32 + n
        return pltpu.make_async_copy(
            yb.at[pl.ds(pl.multiple_of(at * 16, 16), 16)],
            out.at[pl.ds(pl.multiple_of(meta[1 + at] * 16, 16), 16)],
            sems.at[1],
        )

    for q in range(2 * planes):
        x = x_scr[q].reshape(512, 2 * BINS)

        def put(lag, y):
            for h in range(2):
                for c in range(CH_DEV):
                    part = y[c * 64 : c * 64 + 64, h * 128 : h * 128 + 128]
                    if lag + h == 0:
                        at = pl.ds(pl.multiple_of(q * 64, 64), 64)
                        part = jnp.where(first_lane, edge_t[at, c : c + 1], part)
                    if lag + h == 2:
                        kept = d_scr[c * 64 : c * 64 + 64, 256:384].astype(jnp.float32)
                        part = jnp.where(first_lane, kept, part)
                    yf[lag + h, pl.ds(c, 64, stride=8), :] = part
                at = pl.ds((lag + h) * 128, 128)
                yb[pl.ds(pl.multiple_of(q * 512, 512), 512), at] = yf[lag + h].astype(jnp.bfloat16)

        for n in range(2):
            lanes = pl.ds(n * 256, 256)
            even = jnp.dot(x[:, :BINS], e_scr[:BINS, lanes], preferred_element_type=jnp.float32)
            odd = jnp.dot(x[:, BINS:], e_scr[BINS:, lanes], preferred_element_type=jnp.float32)
            put(4 + 2 * n, even + odd)
            d_scr[:, lanes] = (even - odd).astype(jnp.bfloat16)
        put(2, jnp.dot(d_scr[:, :256], flip[:256, 256:], preferred_element_type=jnp.float32))
        put(0, jnp.dot(d_scr[:, 256:], flip[256:, :256], preferred_element_type=jnp.float32))

        for n in range(32):
            copy(q, n).start()

    pltpu.make_async_copy(yb, out.at[pl.ds(0, sources * CH_DEV)], sems.at[1]).wait()


def corr(meta, rows, mine, sib, inverse, out):
    first = out is None
    planes = sum(m.shape[0] for m in mine) // 128
    hbm = pl.BlockSpec(memory_space=pltpu.MemorySpace.HBM)
    args = [meta, rows, *mine, *sib, inverse] + ([] if first else [out])
    return pl.pallas_call(
        lambda *refs: corr_kernel(first, planes, len(mine), *refs),
        out_shape=jax.ShapeDtypeStruct((STEPS * 256 * CH_DEV, NLAG), jnp.bfloat16),
        in_specs=[pl.BlockSpec(memory_space=pltpu.SMEM)] + [hbm] * (len(args) - 1),
        out_specs=hbm,
        scratch_shapes=[
            pltpu.VMEM((2, 4, 32, GROUP), jnp.bfloat16),
            pltpu.VMEM((2, 4, 128 * planes, GROUP), jnp.bfloat16),
            pltpu.VMEM((2 * planes, CH_DEV, 64, 2 * BINS), jnp.bfloat16),
            pltpu.VMEM((2 * BINS, NLAG // 2), jnp.bfloat16),
            pltpu.VMEM((NLAG // 2, NLAG // 2), jnp.bfloat16),
            pltpu.VMEM((2, 16, 128, 128 * planes), jnp.bfloat16),
            pltpu.VMEM((128, 128 * planes), jnp.float32),
            pltpu.VMEM((128 * planes, 128), jnp.float32),
            pltpu.VMEM((512, NLAG // 2), jnp.bfloat16),
            pltpu.VMEM((8, 512, 128), jnp.float32),
            pltpu.VMEM((1024 * planes, NLAG), jnp.bfloat16),
            pltpu.SemaphoreType.DMA((2, 4)),
            pltpu.SemaphoreType.DMA((2,)),
        ],
        input_output_aliases={} if first else {3 + 2 * len(mine): 0},
        compiler_params=pltpu.CompilerParams(vmem_limit_bytes=60 * MIB),
        cost_estimate=pl.CostEstimate(
            flops=planes * 5 * 1024 * 2048 * 1024, bytes_accessed=12 * MIB, transcendentals=0
        ),
        name="corr",
    )(*args)


def device(x, y, z, core):
    return ((z // 2) * 2 + core) * 32 + (z % 2) * 16 + y * 4 + x


def line_pairs(axes, step):
    pairs = []
    for core in range(2):
        for n in range(64):
            at = {"x": n % 4, "y": n // 4 % 4, "z": n // 16}
            to = dict(at)
            to[axes[core]] = (at[axes[core]] + step) % 4
            pairs.append((device(**at, core=core), device(**to, core=core)))
    return pairs


CORE_PAIRS = [
    (device(n % 4, n // 4 % 4, n // 16, core), device(n % 4, n // 4 % 4, n // 16, 1 - core))
    for core in range(2)
    for n in range(64)
]


def line(block, axes):
    return [block] + [lax.ppermute(block, AXES, line_pairs(axes, s)) for s in (1, -1, 2)]


def local(records, channel_map, source_offset):
    forward, inverse = tables()
    forward, inverse = jnp.asarray(forward), jnp.asarray(inverse)
    grp, dev = lax.axis_index("grp"), lax.axis_index("dev")
    core = grp % 2
    x0, y0, z0 = dev % 4, dev // 4 % 4, (grp // 2) * 2 + dev // 16

    pick = (channel_map[0][:, None] == jnp.arange(256, dtype=jnp.int32)[None, :]).astype(jnp.bfloat16)
    pick = lax.optimization_barrier(pick)
    ordered = jnp.dot(pick, records, preferred_element_type=jnp.float32).astype(jnp.bfloat16)
    regrouped = lax.all_to_all(ordered.reshape(32, 8, 512), "dev", split_axis=0, concat_axis=0, tiled=True)

    turns = (4 * core + 2 * jnp.arange(2, dtype=jnp.int32) - source_offset[:, 0]) % 8
    front_meta = jnp.stack([core, turns[0], turns[1]])
    white, keep, send = front(front_meta, regrouped.reshape(8, 4, 8, 512), forward)
    rows = channel_rows(white)
    block = keep + lax.ppermute(send, AXES, CORE_PAIRS)

    near = jnp.concatenate(line(block[None], "xz"), axis=0)
    off = jnp.array(OFFSETS, jnp.int32)
    outer, inner = jnp.meshgrid(off, off, indexing="ij")
    xs = (x0 + jnp.where(core == 0, inner, outer)) % 4
    zs = (z0 + jnp.where(core == 0, outer, inner)) % 4

    def places(offsets):
        ys = (y0 + jnp.array(offsets, jnp.int32).reshape(-1, 1, 1)) % 4
        chip = (zs // 2) * 64 + (zs % 2) * 16 + ys * 4 + xs
        place = chip.reshape(-1, 1, 1) + jnp.arange(2)[None, :, None] * 32 + jnp.arange(2)[None, None, :] * 128
        return jnp.concatenate([core[None], place.reshape(-1)]).astype(jnp.int32)

    def shift(x, step):
        return lax.ppermute(x, AXES, line_pairs("yy", step))

    def swap(xs):
        return [lax.ppermute(x, AXES, CORE_PAIRS) for x in xs]

    def flat(xs):
        return [x.reshape(-1, HALF) for x in xs]

    after = lax.optimization_barrier
    first = line(near, "zx")
    ahead, behind = shift(near, 1), shift(near, -1)
    near, ahead, *first = after((near, ahead, *first))
    second = line(ahead, "zx")
    across = shift(near, 2)
    behind_far = shift(first[3], -1)
    first_sib = swap(first)
    behind, across, *second = after((behind, across, *second))
    both = jnp.concatenate([behind, across], axis=0)
    rest = [both] + [lax.ppermute(both, AXES, line_pairs("zx", s)) for s in (1, -1)]
    across_far = lax.ppermute(across, AXES, line_pairs("zx", 2))
    second_sib = swap(second)
    both_sib = swap([both, behind_far])
    out = corr(places((0, -1)), rows, flat(first + second), flat(first_sib + second_sib), inverse, None)
    out, *rest = after((out, *rest, behind_far, across_far))
    far = swap([rest[1], rest[2], rest[4]])
    rest_sib = [both_sib[0], far[0], far[1], both_sib[1], far[2]]
    out = corr(places((1, 2)), rows, flat(rest), flat(rest_sib), inverse, out)
    return out.reshape(1, STEPS * 256, CH_DEV, NLAG)


def solution(mesh):
    return jax.shard_map(
        local,
        mesh=mesh,
        in_specs=(P("grp", "dev"), P("grp", None), P(None, ("grp", "dev"))),
        out_specs=P(None, None, ("grp", "dev"), None),
        check_vma=False,
    )
```
